128 devices in a mesh: obs: 4 (over z), td: 32 (over y, x, core).
Axes of the slice: x: 4, y: 4, z: 4, core: 2. Of those that a mesh axis runs over, the one named last changes fastest.
Arguments:
- timestreams: bfloat16 [4, 512, 32768], P('obs', 'td'), may hold values from -6 to 6
- filter_taps: bfloat16 [4, 512, 8, 129], P('obs', 'td'), may hold values from -0.5 to 0.5
- scan_bounds: int32 [4, 32], P('obs'), may hold values from 0 to 32768, as said below
- tile_index: int32 [4, 256], P('obs', 'td'), may hold values from 0 to 15
- det_weights: bfloat16 [4, 512], P('obs'), may hold values from 0.29882812 to 3
- positions: float32 [2, 512], replicated, may hold values from -1 to 1
- wafer_group: int32 [512], replicated, may hold values from 0 to 7, as said below
Outputs:
- filtered_residual: float32 [4, 512, 32768], P('obs', 'td')
- sky_map: float32 [16, 128, 128], P(None, ('obs', 'td'))
The draws below stay inside these ranges and needn't reach their ends.
Inputs may be any that keep to these rules, and one draw needn't show every extreme that they name: `scan_bounds`: each row is strictly increasing, starts with 0 and ends with 32768. `wafer_group`: every wafer group holds the same number of detectors.
All inputs are finite; a program needn't handle non-finite values.
Results may differ from the reference program's by a relative error of at most 0.009.
Values may be sent and summed in bfloat16 or wider, within the bound.
No kernel may reach another device: no remote copies, remote signals or barrier semaphores. Data moves between devices by JAX's collectives and lax.ppermute only.
A program may use at most 128 MiB of HBM per device.

```python
import math
import jax
import jax.numpy as jnp
from jax import lax

TAPS = 129
BANDS = 8
TILE = 128
WAFERS = 8
POLY = 6
NINT = 16
OBS = 4
DET = 512
SAMP = 32768
TILES = 16


def draw_wafer_group(key, part):
    order = jax.random.permutation(jax.random.fold_in(key, 17), DET)
    return (order % WAFERS).astype(jnp.int32)


def draw_scan_bounds(key, part):
    keys = jax.random.split(jax.random.fold_in(key, 29), OBS)

    def one_row(row_key):
        inner = jax.random.permutation(row_key, SAMP - 1)[:2 * NINT - 2] + 1
        inner = jnp.sort(inner.astype(jnp.int32))
        return jnp.concatenate([jnp.zeros((1,), jnp.int32), inner, jnp.full((1,), SAMP, jnp.int32)])
    return jax.vmap(one_row)(keys)


def touch_ends(array, rng, low, high):
    shape = array.shape
    place = [jax.random.randint(jax.random.fold_in(rng, axis), (), 0, shape[axis]) for axis in range(len(shape))]
    array = array.at[tuple(place)].set(low)
    longest = shape.index(max(shape))
    place[longest] = (place[longest] + 1) % shape[longest]
    return array.at[tuple(place)].set(high)


def block_scale(stream_key, extent, cuts, smallest, largest):
    factor_of = 1.0
    for position, blocks in cuts:
        steps = jax.random.uniform(jax.random.fold_in(jax.random.fold_in(stream_key, 6), position), (blocks,), jnp.float32, smallest / len(cuts), largest / len(cuts))
        factor_of = factor_of * jnp.repeat(jnp.exp(steps), extent[position] // blocks).reshape((-1,) + (1,) * (len(extent) - 1 - position))
    return factor_of


def noise(rng, extent, width, limit, shards=(), held_as=jnp.bfloat16):
    entries = width * jax.random.normal(rng, extent, jnp.float32)
    if shards:
        entries = entries * block_scale(rng, extent, shards, -0.22, 0.18)
    return jnp.clip(entries, -limit, limit).astype(held_as)


def setup_inputs(seed: int = 0) -> dict:
    streams_of = jax.random.split(jax.random.key(seed), 8)
    return {
        "timestreams": noise(streams_of[0], (OBS, DET, SAMP), 1.0, 6.0, ((0, 4), (1, 32))),
        "filter_taps": noise(streams_of[1], (OBS, DET, BANDS, TAPS), TAPS ** -0.5, 0.5, ((0, 4), (1, 32))),
        "scan_bounds": draw_scan_bounds(jax.random.fold_in(streams_of[7], 71), 0),
        "tile_index": touch_ends(jax.random.randint(streams_of[3], (OBS, SAMP // TILE), 0, TILES), jax.random.fold_in(streams_of[3], 1), 0, TILES - 1).astype(jnp.int32),
        "det_weights": jnp.clip(jnp.exp(math.log(3.0) - 2.306499 * jax.random.uniform(streams_of[4], (OBS, DET), jnp.float32) ** block_scale(streams_of[4], (OBS, DET), ((0, 4),), -0.2, 0.2)), 0.29882812, 3.0).astype(jnp.bfloat16),
        "positions": jnp.clip(jax.random.uniform(streams_of[5], (2, DET), jnp.float32, -1.0, 1.0), -1.0, 1.0),
        "wafer_group": draw_wafer_group(jax.random.fold_in(streams_of[7], 71), 0),
    }


prior_weight = 1.0

def toeplitz(band_taps):
    leading = band_taps.shape[:-1]
    half = TAPS // 2
    padded = jnp.concatenate([jnp.zeros(leading + (TILE - half,), band_taps.dtype), band_taps, jnp.zeros(leading + (3 * TILE - TAPS + half,), band_taps.dtype)], axis=-1)
    repeated = jnp.tile(padded, (1,) * len(leading) + (TILE,))
    repeated = repeated[..., :TILE * (4 * TILE - 1)].reshape(leading + (TILE, 4 * TILE - 1))
    return repeated[..., :3 * TILE]

def windows_of(signal):
    blocks = jnp.pad(signal, ((0, 0), (0, 0), (TILE, TILE)))
    blocks = blocks.reshape(signal.shape[0], signal.shape[1], -1, TILE)
    return jnp.concatenate([blocks[:, :, :-2], blocks[:, :, 1:-1], blocks[:, :, 2:]], axis=-1)

def forward_filter(signal, filter_taps):
    windows = windows_of(signal)
    per_band = windows.shape[2] // BANDS
    pieces = []
    for band_idx in range(BANDS):
        kernel = toeplitz(filter_taps[:, :, band_idx]).astype(jnp.float32)
        band_part = windows[:, :, band_idx * per_band:(band_idx + 1) * per_band].astype(jnp.float32)
        pieces.append(jnp.einsum('odnj,odij->odni', band_part, kernel, precision=lax.Precision.HIGHEST))
    return jnp.concatenate(pieces, axis=2).reshape(signal.shape)

def adjoint_filter(signal, filter_taps):
    blocks = signal.reshape(signal.shape[0], signal.shape[1], -1, TILE)
    per_band = blocks.shape[2] // BANDS
    pieces = []
    for band_idx in range(BANDS):
        kernel = toeplitz(filter_taps[:, :, band_idx]).astype(jnp.float32)
        band_part = blocks[:, :, band_idx * per_band:(band_idx + 1) * per_band].astype(jnp.float32)
        pieces.append(jnp.einsum('odni,odij->odnj', band_part, kernel, precision=lax.Precision.HIGHEST))
    spread = jnp.concatenate(pieces, axis=2)
    zero_block = jnp.zeros(spread.shape[:2] + (1, TILE), jnp.float32)
    from_next = jnp.concatenate([spread[:, :, 1:, :TILE], zero_block], axis=2)
    from_prev = jnp.concatenate([zero_block, spread[:, :, :-1, 2 * TILE:]], axis=2)
    summed = spread[:, :, :, TILE:2 * TILE] + from_next + from_prev
    return summed.reshape(signal.shape)

def make_basis(positions, wafer_group):
    x_pos = positions[0]
    y_pos = positions[1]
    monomials = jnp.stack([jnp.ones_like(x_pos), x_pos, y_pos, x_pos * x_pos, x_pos * y_pos, y_pos * y_pos])
    member = (wafer_group[None, :] == jnp.arange(WAFERS, dtype=jnp.int32)[:, None]).astype(jnp.float32)
    basis_b = (member[:, None, :] * monomials[None]).reshape(WAFERS * POLY, -1).astype(jnp.bfloat16)
    basis_f = basis_b.astype(jnp.float32)
    gram_matrix = jnp.dot(basis_f, basis_f.T, precision=lax.Precision.HIGHEST)
    factor = jnp.linalg.cholesky(gram_matrix)
    lower_inv = lax.linalg.triangular_solve(factor, jnp.eye(WAFERS * POLY, dtype=jnp.float32), left_side=True, lower=True)
    inverse = jnp.dot(lower_inv.T, lower_inv, precision=lax.Precision.HIGHEST)
    return (basis_b, basis_f, inverse)

def remove_poly(gathered, basis):
    basis_b, basis_f, inverse = basis
    coef_raw = jnp.einsum('md,nds->nms', basis_f, gathered.astype(jnp.float32), precision=lax.Precision.HIGHEST)
    coefficients = jnp.einsum('mq,nqs->nms', inverse, coef_raw, precision=lax.Precision.HIGHEST)
    fitted = jnp.einsum('md,nms->nds', basis_f, coefficients, precision=lax.Precision.HIGHEST)
    return (gathered.astype(jnp.float32) - fitted).astype(jnp.bfloat16)

def scan_flags(bounds, offset, length):
    sample = offset + jnp.arange(length, dtype=jnp.int32)
    passed = jnp.sum((bounds[:, :, None] <= sample[None, None, :]).astype(jnp.int32), axis=1)
    return (passed % 2).astype(jnp.float32)

def bin_maps(cleaned, in_scan, det_weights, tile_index):
    obs_count, det_count, samples = cleaned.shape
    groups = det_count // TILE
    block_count = samples // TILE
    masked = cleaned.astype(jnp.float32) * in_scan[:, None, :]
    shaped = masked.reshape(obs_count, groups, TILE, block_count, TILE)
    weight_rows = det_weights.astype(jnp.float32).reshape(obs_count, groups, TILE)
    block_sums = jnp.einsum('oqr,oqrbc->obrc', weight_rows, shaped, precision=lax.Precision.HIGHEST)
    row_weight = jnp.sum(weight_rows, axis=1)
    one_hot = (tile_index[:, :, None] == jnp.arange(TILES, dtype=jnp.int32)[None, None, :]).astype(jnp.float32)
    weighted_sum = jnp.einsum('obt,obrc->trc', one_hot, block_sums, precision=lax.Precision.HIGHEST)
    scan_blocks = in_scan.reshape(obs_count, block_count, TILE)
    hit_weight = jnp.einsum('obt,or,obc->trc', one_hot, row_weight, scan_blocks, precision=lax.Precision.HIGHEST)
    return (weighted_sum, hit_weight, one_hot)

def rescan_residual(cleaned, in_scan, sky_b, one_hot):
    obs_count, det_count, samples = cleaned.shape
    groups = det_count // TILE
    block_count = samples // TILE
    selected = jnp.einsum('obt,trc->orbc', one_hot, sky_b.astype(jnp.float32), precision=lax.Precision.HIGHEST)
    shaped = cleaned.astype(jnp.float32).reshape(obs_count, groups, TILE, block_count, TILE)
    deviation = shaped - selected[:, None]
    flags = in_scan.reshape(obs_count, 1, 1, block_count, TILE)
    return (flags * deviation).astype(jnp.bfloat16).reshape(obs_count, det_count, samples)

def reference(timestreams, filter_taps, scan_bounds, tile_index, det_weights, positions, wafer_group):
    basis = make_basis(positions, wafer_group)
    weighted_sum = jnp.zeros((TILES, TILE, TILE), jnp.float32)
    hit_weight = jnp.zeros((TILES, TILE, TILE), jnp.float32)
    kept = []
    for obs_idx in range(OBS):
        filtered = forward_filter(timestreams[obs_idx:obs_idx + 1], filter_taps[obs_idx:obs_idx + 1]).astype(jnp.bfloat16)
        cleaned = remove_poly(filtered, basis)
        in_scan = scan_flags(scan_bounds[obs_idx:obs_idx + 1], 0, SAMP)
        part_sum, part_hit, one_hot = bin_maps(cleaned, in_scan, det_weights[obs_idx:obs_idx + 1], tile_index[obs_idx:obs_idx + 1])
        weighted_sum = weighted_sum + part_sum
        hit_weight = hit_weight + part_hit
        kept.append((cleaned, in_scan, one_hot))
    sky_map = weighted_sum / (hit_weight + prior_weight)
    sky_b = sky_map.astype(jnp.bfloat16)
    outputs = []
    for obs_idx in range(OBS):
        cleaned, in_scan, one_hot = kept[obs_idx]
        residual = rescan_residual(cleaned, in_scan, sky_b, one_hot)
        outputs.append(adjoint_filter(residual, filter_taps[obs_idx:obs_idx + 1]))
    return (jnp.concatenate(outputs, axis=0), sky_map)
```

```python
import functools

import jax
import jax.numpy as jnp
from jax import lax
from jax.experimental import pallas as pl
from jax.experimental.pallas import tpu as pltpu
from jax.sharding import Mesh
from jax.sharding import PartitionSpec as P

TAPS = 129
BANDS = 8
TILE = 128
WAFERS = 8
POLY = 6
NINT = 16
OBS = 4
DET = 512
SAMP = 32768
TILES = 16

QUADS = 4
GROUPS = 8
ROWS = 16
BLOCKS = SAMP // TILE
SLABS = QUADS * GROUPS
SLAB_BLOCKS = BLOCKS // SLABS
BAND_BLOCKS = BLOCKS // BANDS
HALF = TILE // 2
GROUP_AXES = ("obs", "q")
SLAB_AXES = ("q", "g")
ALL_AXES = ("obs", "q", "g")

prior_weight = 1.0
VMEM_LIMIT = 48 * 1024 * 1024


def vmem():
    return pl.BlockSpec(memory_space=pltpu.VMEM)


def smem():
    return pl.BlockSpec(memory_space=pltpu.SMEM)


def call(kernel, out_shape, in_specs, out_specs, scratch=(), flops=0, bytes_accessed=0):
    return pl.pallas_call(
        kernel,
        out_shape=out_shape,
        in_specs=in_specs,
        out_specs=out_specs,
        scratch_shapes=list(scratch),
        compiler_params=pltpu.CompilerParams(vmem_limit_bytes=VMEM_LIMIT),
        cost_estimate=pl.CostEstimate(flops=flops, bytes_accessed=bytes_accessed, transcendentals=0),
    )


def lane_ids(shape):
    return lax.broadcasted_iota(jnp.int32, shape, len(shape) - 1)


def row_ids(shape):
    return lax.broadcasted_iota(jnp.int32, shape, len(shape) - 2)


def circulant(row):
    return pltpu.roll(jnp.broadcast_to(row, (TILE, TILE)), 0, 1, stride=1, stride_axis=0)


def forward_kernel(x_ref, taps_ref, y_ref, shifted, summed, first, last):
    taps = taps_ref[...].astype(jnp.float32)
    head = taps[:, :, :TILE].reshape(ROWS * BANDS, TILE).astype(jnp.bfloat16)
    reverse = (row_ids((TILE, TILE)) == ((TILE - lane_ids((TILE, TILE))) & (TILE - 1))).astype(
        jnp.float32
    )
    first[...] = jnp.dot(head, reverse.astype(jnp.bfloat16), preferred_element_type=jnp.float32)
    last[...] = jnp.broadcast_to(taps[:, :, TILE:], (ROWS, BANDS, TILE)).reshape(
        ROWS * BANDS, TILE
    )
    low = lane_ids((ROWS, TILE)) < HALF

    def shift_slab(slab, before):
        for inner in range(SLAB_BLOCKS):
            block = slab * SLAB_BLOCKS + inner
            start = pl.multiple_of(block * TILE, TILE)
            here = pltpu.roll(x_ref[0, :, pl.ds(start, TILE)].astype(jnp.float32), HALF, 1)
            shifted[pl.ds(pl.multiple_of(block * ROWS, ROWS), ROWS), :] = jnp.where(
                low, before, here
            )
            before = here
        return before

    before = lax.fori_loop(0, SLABS, shift_slab, jnp.zeros((ROWS, TILE), jnp.float32))
    shifted[BLOCKS * ROWS :, :] = jnp.where(low, before, 0.0)

    rows, lanes = row_ids((TILE, TILE)), lane_ids((TILE, TILE))
    in_first = lanes <= rows
    on_diag = lanes == rows

    def one_detector(det, carry):
        for band in range(BANDS):
            pair = det * BANDS + band
            turned = circulant(first[pl.ds(pair, 1), :])
            end = jnp.broadcast_to(last[pl.ds(pair, 1), :], (TILE, TILE))
            upper = jnp.where(in_first, turned, 0.0)
            lower = jnp.where(in_first, jnp.where(on_diag, end, 0.0), turned)
            kernel = jnp.concatenate([upper, lower], axis=0).astype(jnp.bfloat16)
            base = band * BAND_BLOCKS * ROWS + det
            one = shifted[pl.ds(base, BAND_BLOCKS, stride=ROWS), :]
            two = shifted[pl.ds(base + ROWS, BAND_BLOCKS, stride=ROWS), :]
            window = jnp.concatenate([one, two], axis=1).astype(jnp.bfloat16)
            summed[pl.ds(base, BAND_BLOCKS, stride=ROWS), :] = jnp.dot(
                window, kernel, preferred_element_type=jnp.float32
            )
        return carry

    lax.fori_loop(0, ROWS, one_detector, 0)

    def write_slab(slab, carry):
        for inner in range(SLAB_BLOCKS):
            block = slab * SLAB_BLOCKS + inner
            part = summed[pl.ds(pl.multiple_of(block * ROWS, ROWS), ROWS), :]
            y_ref[slab, :, inner * TILE : (inner + 1) * TILE] = part.astype(jnp.bfloat16)
        return carry

    lax.fori_loop(0, SLABS, write_slab, 0)


def clean_kernel(data_ref, basis_ref, basis_t_ref, inverse_ref, out_ref):
    data = data_ref[...].reshape(DET, SLAB_BLOCKS * TILE)
    raw = jnp.dot(basis_ref[...], data, preferred_element_type=jnp.float32)
    coef = jnp.dot(
        inverse_ref[...],
        raw,
        precision=lax.Precision.HIGHEST,
        preferred_element_type=jnp.float32,
    )
    high = coef.astype(jnp.bfloat16)
    rest = (coef - high.astype(jnp.float32)).astype(jnp.bfloat16)
    both = jnp.concatenate([high, rest], axis=0)
    fitted = jnp.dot(basis_t_ref[...], both, preferred_element_type=jnp.float32)
    out = (data.astype(jnp.float32) - fitted).astype(jnp.bfloat16)
    out_ref[...] = out.reshape(out_ref.shape)


def write_flags(flags, bounds_ref, obs):
    for part in range(BANDS):
        sample = (
            (row_ids((BAND_BLOCKS, TILE)) + part * BAND_BLOCKS) * TILE
            + lane_ids((BAND_BLOCKS, TILE))
        )
        passed = jnp.zeros((BAND_BLOCKS, TILE), jnp.int32)
        for bound in range(2 * NINT):
            passed = passed + (bounds_ref[obs, bound] <= sample).astype(jnp.int32)
        flags[part * BAND_BLOCKS : (part + 1) * BAND_BLOCKS, :] = (passed & 1).astype(jnp.float32)


def hits_kernel(bounds_ref, tiles_ref, weight_ref, out_ref, flags):
    sums = []
    for obs in range(OBS):
        write_flags(flags, bounds_ref, obs)
        chosen = row_ids((TILES, BLOCKS)) == tiles_ref[obs : obs + 1, :]
        sums.append(
            jnp.dot(
                chosen.astype(jnp.bfloat16),
                flags[...].astype(jnp.bfloat16),
                preferred_element_type=jnp.float32,
            )
        )
    for tile in range(TILES):
        total = jnp.zeros((ROWS, TILE), jnp.float32)
        for obs in range(OBS):
            total = total + weight_ref[obs] * sums[obs][tile : tile + 1, :]
        out_ref[tile] = total


def bin_kernel(bounds_ref, tiles_ref, data_ref, weight_ref, out_ref, flags):
    write_flags(flags, bounds_ref, 0)
    out_ref[...] = jnp.zeros_like(out_ref)

    def add_slab(slab, carry):
        for inner in range(SLAB_BLOCKS):
            block = slab * SLAB_BLOCKS + inner
            part = data_ref[slab, :, inner * TILE : (inner + 1) * TILE].astype(jnp.float32)
            tile = tiles_ref[block]
            out_ref[tile] = out_ref[tile] + part * flags[pl.ds(block, 1), :]
        return carry

    lax.fori_loop(0, SLABS, add_slab, 0)
    for tile in range(TILES):
        out_ref[tile] = out_ref[tile] * weight_ref[...]


def adjoint_kernel(
    bounds_ref, tiles_ref, data_ref, sky_ref, taps_ref, out_ref, flags, resid, same, after, first, last
):
    write_flags(flags, bounds_ref, 0)
    taps = taps_ref[...].astype(jnp.float32)
    first[...] = taps[:, :, :TILE].reshape(ROWS * BANDS, TILE)
    last[...] = jnp.broadcast_to(taps[:, :, TILE:], (ROWS, BANDS, TILE)).reshape(
        ROWS * BANDS, TILE
    )

    def residual_slab(slab, carry):
        for inner in range(SLAB_BLOCKS):
            block = slab * SLAB_BLOCKS + inner
            part = data_ref[slab, :, inner * TILE : (inner + 1) * TILE].astype(jnp.float32)
            sky = sky_ref[tiles_ref[block]].astype(jnp.bfloat16).astype(jnp.float32)
            value = flags[pl.ds(block, 1), :] * (part - sky)
            resid[pl.ds(pl.multiple_of(block * ROWS, ROWS), ROWS), :] = value
        return carry

    lax.fori_loop(0, SLABS, residual_slab, 0)

    rows, lanes = row_ids((TILE, TILE)), lane_ids((TILE, TILE))
    in_first = lanes >= rows
    on_diag = lanes == rows
    after[:ROWS, :] = jnp.zeros((ROWS, TILE), jnp.float32)

    def one_detector(det, carry):
        for band in range(BANDS):
            pair = det * BANDS + band
            turned = circulant(first[pl.ds(pair, 1), :])
            end = jnp.broadcast_to(last[pl.ds(pair, 1), :], (TILE, TILE))
            upper = jnp.where(in_first, turned, 0.0)
            lower = jnp.where(in_first, jnp.where(on_diag, end, 0.0), turned)
            kernel = jnp.concatenate([upper, lower], axis=1).astype(jnp.bfloat16)
            base = band * BAND_BLOCKS * ROWS + det
            part = resid[pl.ds(base, BAND_BLOCKS, stride=ROWS), :].astype(jnp.bfloat16)
            spread = jnp.dot(part, kernel, preferred_element_type=jnp.float32)
            same[pl.ds(base, BAND_BLOCKS, stride=ROWS), :] = spread[:, :TILE]
            after[pl.ds(base + ROWS, BAND_BLOCKS, stride=ROWS), :] = spread[:, TILE:]
        return carry

    lax.fori_loop(0, ROWS, one_detector, 0)
    same[BLOCKS * ROWS :, :] = jnp.zeros((ROWS, TILE), jnp.float32)
    low = lane_ids((ROWS, TILE)) < HALF

    def joined(block):
        start = pl.multiple_of(block * ROWS, ROWS)
        return pltpu.roll(same[pl.ds(start, ROWS), :] + after[pl.ds(start, ROWS), :], HALF, 1)

    def write_slab(slab, here):
        for inner in range(SLAB_BLOCKS):
            block = slab * SLAB_BLOCKS + inner
            following = joined(block + 1)
            out_ref[0, :, pl.ds(pl.multiple_of(block * TILE, TILE), TILE)] = jnp.where(
                low, here, following
            )
            here = following
        return here

    lax.fori_loop(0, SLABS, write_slab, joined(0))


def make_basis(positions, wafer_group):
    x_pos = positions[0]
    y_pos = positions[1]
    monomials = jnp.stack(
        [jnp.ones_like(x_pos), x_pos, y_pos, x_pos * x_pos, x_pos * y_pos, y_pos * y_pos]
    )
    member = (wafer_group[None, :] == jnp.arange(WAFERS, dtype=jnp.int32)[:, None]).astype(
        jnp.float32
    )
    basis_b = (member[:, None, :] * monomials[None]).reshape(WAFERS * POLY, -1).astype(jnp.bfloat16)
    basis_f = basis_b.astype(jnp.float32)
    gram_matrix = jnp.dot(basis_f, basis_f.T, precision=lax.Precision.HIGHEST)
    factor = jnp.linalg.cholesky(gram_matrix)
    lower_inv = lax.linalg.triangular_solve(
        factor, jnp.eye(WAFERS * POLY, dtype=jnp.float32), left_side=True, lower=True
    )
    inverse = jnp.dot(lower_inv.T, lower_inv, precision=lax.Precision.HIGHEST)
    return (basis_b, inverse)


def exchange(value, axis):
    size = lax.axis_size(axis)
    return [
        lax.ppermute(value, axis, [(src, (src + step) % size) for src in range(size)])
        for step in range(1, size)
    ]


def local(timestreams, filter_taps, scan_bounds, tile_index, det_weights, positions, wafer_group):
    f32 = jnp.float32
    shape = jax.ShapeDtypeStruct
    obs = lax.axis_index("obs")
    group = lax.axis_index("g")
    slab = lax.axis_index(SLAB_AXES)
    taps = filter_taps.reshape(ROWS, BANDS, TAPS)
    own_weights = lax.dynamic_slice_in_dim(det_weights[0], slab * ROWS, ROWS).astype(f32)
    own_bound = lax.dynamic_slice_in_dim(scan_bounds[0], slab, 1).astype(f32)
    pieces = [tile_index[0].astype(f32), own_bound, own_weights]
    used = SLAB_BLOCKS + 1 + ROWS
    meta = jnp.concatenate(pieces + [jnp.zeros((TILE - used,), f32)]).reshape(1, TILE)
    meta = lax.all_gather(meta, ALL_AXES, axis=0, tiled=True).reshape(OBS, SLABS, TILE)
    all_tiles = meta[:, :, :SLAB_BLOCKS].reshape(OBS, BLOCKS).astype(jnp.int32)
    all_bounds = meta[:, :, SLAB_BLOCKS].astype(jnp.int32)
    all_weights = meta[:, :, SLAB_BLOCKS + 1 : used].reshape(OBS, QUADS, GROUPS, ROWS)
    row_weights = jnp.sum(lax.dynamic_index_in_dim(all_weights, group, 2, keepdims=False), axis=1)
    own_tiles = lax.dynamic_index_in_dim(all_tiles, obs, 0, keepdims=False)

    filtered = call(
        forward_kernel,
        shape((SLABS, ROWS, SLAB_BLOCKS * TILE), jnp.bfloat16),
        [vmem(), vmem()],
        vmem(),
        [
            pltpu.VMEM(((BLOCKS + 1) * ROWS, TILE), f32),
            pltpu.VMEM((BLOCKS * ROWS, TILE), f32),
            pltpu.VMEM((ROWS * BANDS, TILE), f32),
            pltpu.VMEM((ROWS * BANDS, TILE), f32),
        ],
    )(timestreams, taps)
    basis, inverse = make_basis(positions, wafer_group)
    gathered = lax.all_to_all(filtered, SLAB_AXES, split_axis=0, concat_axis=0, tiled=True)
    cleaned = call(
        clean_kernel,
        shape((SLABS, ROWS, SLAB_BLOCKS * TILE), jnp.bfloat16),
        [vmem()] * 4,
        vmem(),
    )(gathered, basis, jnp.concatenate([basis, basis], axis=0).T, inverse)
    returned = lax.all_to_all(cleaned, SLAB_AXES, split_axis=0, concat_axis=0, tiled=True)

    hits = call(
        hits_kernel,
        shape((TILES, ROWS, TILE), f32),
        [smem(), vmem(), vmem()],
        vmem(),
        [pltpu.VMEM((BLOCKS, TILE), f32)],
    )(all_bounds, all_tiles, jnp.broadcast_to(row_weights[:, :, None], (OBS, ROWS, TILE)))
    part = call(
        bin_kernel,
        shape((TILES, ROWS, TILE), f32),
        [smem(), smem(), vmem(), vmem()],
        vmem(),
        [pltpu.VMEM((BLOCKS, TILE), f32)],
    )(scan_bounds, own_tiles, returned, jnp.broadcast_to(own_weights[:, None], (ROWS, TILE)))
    part = sum(exchange(part, "obs"), part)
    part = sum(exchange(part, "q"), part)
    sky = part / (hits + prior_weight)
    row = lax.axis_index(GROUP_AXES)
    sky_row = lax.dynamic_slice_in_dim(sky, row, 1, 1)
    moves = [
        ((o * QUADS + q) * GROUPS + g, g * ROWS + o * QUADS + q)
        for o in range(OBS)
        for q in range(QUADS)
        for g in range(GROUPS)
    ]
    sky_own = lax.ppermute(sky_row, ALL_AXES, moves)
    out = call(
        adjoint_kernel,
        shape((1, ROWS, SAMP), f32),
        [smem(), smem(), vmem(), vmem(), vmem()],
        vmem(),
        [
            pltpu.VMEM((BLOCKS, TILE), f32),
            pltpu.VMEM((BLOCKS * ROWS, TILE), f32),
            pltpu.VMEM(((BLOCKS + 1) * ROWS, TILE), f32),
            pltpu.VMEM(((BLOCKS + 1) * ROWS, TILE), f32),
            pltpu.VMEM((ROWS * BANDS, TILE), f32),
            pltpu.VMEM((ROWS * BANDS, TILE), f32),
        ],
    )(scan_bounds, own_tiles, returned, sky, taps)
    return (out, sky_own)


def solution(mesh):
    split = Mesh(mesh.devices.reshape(OBS, QUADS, GROUPS), ALL_AXES)
    placed = (
        P("obs", SLAB_AXES, None),
        P("obs", SLAB_AXES, None, None),
        P("obs", None),
        P("obs", SLAB_AXES),
        P("obs", None),
        P(),
        P(),
    )
    return jax.shard_map(
        local,
        mesh=split,
        in_specs=placed,
        out_specs=(P("obs", SLAB_AXES, None), P(None, ALL_AXES, None)),
        check_vma=False,
    )
```

```python
import functools

import jax
import jax.numpy as jnp
from jax import lax
from jax.experimental import pallas as pl
from jax.experimental.pallas import tpu as pltpu
from jax.sharding import Mesh
from jax.sharding import PartitionSpec as P

TAPS = 129
BANDS = 8
TILE = 128
WAFERS = 8
POLY = 6
NINT = 16
OBS = 4
DET = 512
SAMP = 32768
TILES = 16

QUADS = 4
GROUPS = 8
ROWS = 16
BLOCKS = SAMP // TILE
SLABS = QUADS * GROUPS
SLAB_BLOCKS = BLOCKS // SLABS
BAND_BLOCKS = BLOCKS // BANDS
HALF = TILE // 2
GROUP_AXES = ("obs", "q")
SLAB_AXES = ("q", "g")
ALL_AXES = ("obs", "q", "g")

prior_weight = 1.0
MIB = 1024 * 1024
BAND_SLABS = SLABS // BANDS
SLAB_LEN = SLAB_BLOCKS * TILE
SHARE = TILE // SLABS
SUM_ROWS = TILES * SHARE


def vmem():
    return pl.BlockSpec(memory_space=pltpu.VMEM)


def smem():
    return pl.BlockSpec(memory_space=pltpu.SMEM)


def hbm():
    return pl.BlockSpec(memory_space=pltpu.HBM)


def call(kernel, out_shape, in_specs, out_specs, scratch=(), limit=32, micros=2):
    return pl.pallas_call(
        kernel,
        out_shape=out_shape,
        in_specs=in_specs,
        out_specs=out_specs,
        scratch_shapes=list(scratch),
        compiler_params=pltpu.CompilerParams(vmem_limit_bytes=limit * MIB),
        cost_estimate=pl.CostEstimate(
            flops=0, bytes_accessed=micros * 3_000_000, transcendentals=0
        ),
    )


def lane_ids(shape):
    return lax.broadcasted_iota(jnp.int32, shape, len(shape) - 1)


def row_ids(shape):
    return lax.broadcasted_iota(jnp.int32, shape, len(shape) - 2)


def circulant(row):
    return pltpu.roll(jnp.broadcast_to(row, (TILE, TILE)), 0, 1, stride=1, stride_axis=0)


def start(block, size):
    return pl.multiple_of(block * size, size)


def forward_kernel(
    x_ref, taps_ref, meta_ref, y_ref, x_buf, taps_buf, shifted, summed, y_buf, first, last, sems
):
    taps_copy = pltpu.make_async_copy(taps_ref, taps_buf, sems.at[0, BANDS])
    taps_copy.start()

    def x_copy(band):
        part = pl.ds(start(band, BAND_BLOCKS * TILE), BAND_BLOCKS * TILE)
        return pltpu.make_async_copy(x_ref.at[0, :, part], x_buf.at[:, part], sems.at[0, band])

    def y_copy(band):
        part = pl.ds(band * BAND_SLABS, BAND_SLABS)
        return pltpu.make_async_copy(y_buf.at[part], y_ref.at[part], sems.at[1, band])

    for band in range(BANDS):
        x_copy(band).start()
    low = lane_ids((ROWS, TILE)) < HALF
    rows, lanes = row_ids((TILE, TILE)), lane_ids((TILE, TILE))
    in_first = lanes <= rows
    on_diag = lanes == rows
    reverse = (rows == ((TILE - lanes) & (TILE - 1))).astype(jnp.float32).astype(jnp.bfloat16)
    taps_copy.wait()
    taps = taps_buf[...].astype(jnp.float32)
    front = taps[:, :, :TILE].reshape(ROWS * BANDS, TILE).astype(jnp.bfloat16)
    first[...] = jnp.dot(front, reverse, preferred_element_type=jnp.float32)
    last[...] = jnp.broadcast_to(taps[:, :, TILE:], (ROWS, BANDS, TILE)).reshape(
        ROWS * BANDS, TILE
    )

    def rolled(block):
        part = x_buf[:, pl.ds(start(block, TILE), TILE)]
        return pltpu.roll(part.astype(jnp.float32), HALF, 1)

    x_copy(0).wait()
    opening = rolled(0)
    shifted[:ROWS, :] = jnp.where(low, 0.0, opening)

    def one_band(band, before):
        @pl.when(band < BANDS - 1)
        def _():
            x_copy(band + 1).wait()

        for inner in range(1, BAND_BLOCKS + 1):
            block = band * BAND_BLOCKS + inner
            if inner == BAND_BLOCKS:
                here = jnp.where(
                    band < BANDS - 1, rolled(jnp.minimum(block, BLOCKS - 1)), 0.0
                )
            else:
                here = rolled(block)
            shifted[pl.ds(start(block, ROWS), ROWS), :] = jnp.where(low, before, here)
            before = here
        for det in range(ROWS):
            pair = det * BANDS + band
            turned = circulant(first[pl.ds(pair, 1), :])
            end = jnp.broadcast_to(last[pl.ds(pair, 1), :], (TILE, TILE))
            upper = jnp.where(in_first, turned, 0.0)
            lower = jnp.where(in_first, jnp.where(on_diag, end, 0.0), turned)
            kernel = jnp.concatenate([upper, lower], axis=0).astype(jnp.bfloat16)
            base = band * BAND_BLOCKS * ROWS + det
            one = shifted[pl.ds(base, BAND_BLOCKS, stride=ROWS), :]
            two = shifted[pl.ds(base + ROWS, BAND_BLOCKS, stride=ROWS), :]
            window = jnp.concatenate([one, two], axis=1).astype(jnp.bfloat16)
            summed[pl.ds(base, BAND_BLOCKS, stride=ROWS), :] = jnp.dot(
                window, kernel, preferred_element_type=jnp.float32
            )
        for part in range(BAND_SLABS):
            slab = band * BAND_SLABS + part
            for inner in range(SLAB_BLOCKS):
                block = slab * SLAB_BLOCKS + inner
                y_buf[slab, :, inner * TILE : (inner + 1) * TILE] = summed[
                    pl.ds(start(block, ROWS), ROWS), :
                ].astype(jnp.bfloat16)
            y_buf[slab, :, SLAB_LEN:] = meta_ref[...]
        y_copy(band).start()
        return before

    lax.fori_loop(0, BANDS, one_band, opening)
    for band in range(BANDS):
        y_copy(band).wait()


def count_flags(bounds_ref, blocks, offset):
    sample = (row_ids((blocks, TILE)) + offset) * TILE + lane_ids((blocks, TILE))
    passed = jnp.zeros((blocks, TILE), jnp.int32)
    for bound in range(2 * NINT):
        passed = passed + (bounds_ref[0, bound] <= sample).astype(jnp.int32)
    return (passed & 1).astype(jnp.float32)


def clean_kernel(
    bounds_ref, data_ref, basis_ref, basis_t_ref, inverse_ref, weight_ref, out_ref, sums_ref, tiles_ref
):
    data = data_ref[:, :, :SLAB_LEN].reshape(DET, SLAB_LEN)
    tiles_ref[...] = data_ref[:, :, SLAB_LEN:].astype(jnp.float32)[:, 0, :].astype(jnp.int32)
    raw = jnp.dot(basis_ref[...], data, preferred_element_type=jnp.float32)
    coef = jnp.dot(
        inverse_ref[...],
        raw,
        precision=lax.Precision.HIGHEST,
        preferred_element_type=jnp.float32,
    )
    high = coef.astype(jnp.bfloat16)
    rest = (coef - high.astype(jnp.float32)).astype(jnp.bfloat16)
    both = jnp.concatenate([high, rest], axis=0)
    fitted = jnp.dot(basis_t_ref[...], both, preferred_element_type=jnp.float32)
    cleaned = (data.astype(jnp.float32) - fitted).astype(jnp.bfloat16)
    out_ref[...] = cleaned.reshape(out_ref.shape)
    flags = count_flags(bounds_ref, SLAB_BLOCKS, 0)
    for block in range(SLAB_BLOCKS):
        part = cleaned[:, block * TILE : (block + 1) * TILE].astype(jnp.float32)
        weighted = (part * weight_ref[...]).reshape(DET // TILE, TILE, TILE)
        total = jnp.sum(weighted, axis=0) * flags[block : block + 1, :]
        for quad in range(QUADS):
            for group in range(GROUPS):
                row = group * ROWS + quad * SHARE
                sums_ref[quad * GROUPS + group, block * SHARE : (block + 1) * SHARE, :] = total[
                    row : row + SHARE, :
                ]


def scan_kernel(bounds_ref, tiles_ref, weight_ref, flags_ref, scan_ref, acc):
    for band in range(BANDS):
        flags_ref[band * BAND_BLOCKS : (band + 1) * BAND_BLOCKS, :] = count_flags(
            bounds_ref, BAND_BLOCKS, band * BAND_BLOCKS
        )
    acc[...] = jnp.zeros_like(acc)

    def add_slab(slab, carry):
        for inner in range(SLAB_BLOCKS):
            tile = tiles_ref[slab, inner]
            row = flags_ref[pl.ds(slab * SLAB_BLOCKS + inner, 1), :]
            acc[tile] = acc[tile] + jnp.broadcast_to(row, (8, TILE))
        return carry

    lax.fori_loop(0, SLABS, add_slab, 0)
    for tile in range(TILES):
        scan_ref[tile : tile + 1, :] = acc[tile, :1, :]
    scan_ref[TILES:, :] = weight_ref[...]


def bin_kernel(tiles_ref, sums_ref, scan_ref, out_ref, acc):
    acc[...] = jnp.zeros_like(acc)
    upper = row_ids((2 * SHARE, TILE)) < SHARE

    def add_slab(slab, carry):
        for pair in range(SLAB_BLOCKS // 2):
            part = sums_ref[slab, pair * 2 * SHARE : (pair + 1) * 2 * SHARE, :]
            even = tiles_ref[slab, 2 * pair]
            acc[even] = acc[even] + jnp.where(upper, part, 0.0)
            odd = tiles_ref[slab, 2 * pair + 1]
            acc[odd] = acc[odd] + jnp.where(upper, 0.0, part)
        return carry

    lax.fori_loop(0, SLABS, add_slab, 0)
    for tile in range(TILES):
        both = acc[tile]
        out_ref[tile * SHARE : (tile + 1) * SHARE, :] = both[:SHARE, :] + both[SHARE:, :]
    out_ref[SUM_ROWS:, :] = scan_ref[...]


def sky_kernel(a_ref, b_ref, c_ref, d_ref, sky_ref, sky_b_ref):
    refs = (a_ref, b_ref, c_ref, d_ref)
    upper = row_ids((2 * SHARE, TILE)) < SHARE
    weights = [ref[SUM_ROWS + TILES :, :] for ref in refs]
    for pair in range(TILES // 2):
        rows = slice(pair * 2 * SHARE, (pair + 1) * 2 * SHARE)
        total = jnp.zeros((2 * SHARE, TILE), jnp.float32)
        hits = jnp.zeros((2 * SHARE, TILE), jnp.float32)
        for ref, weight in zip(refs, weights):
            total = total + ref[rows, :]
            even = ref[SUM_ROWS + 2 * pair : SUM_ROWS + 2 * pair + 1, :]
            odd = ref[SUM_ROWS + 2 * pair + 1 : SUM_ROWS + 2 * pair + 2, :]
            hits = hits + weight * jnp.where(upper, even, odd)
        sky_ref[rows, :] = total / (hits + prior_weight)
    sky_b_ref[...] = sky_ref[...].astype(jnp.bfloat16)


def adjoint_kernel(
    tiles_ref, flags_ref, data_ref, sky_ref, taps_ref, out_ref, sky, resid, same, after, out_buf, first, last, sems
):
    def out_copy(band):
        part = pl.ds(start(band, BAND_BLOCKS * TILE), BAND_BLOCKS * TILE)
        return pltpu.make_async_copy(out_buf.at[:, part], out_ref.at[0, :, part], sems.at[band])

    sky[...] = sky_ref[...].astype(jnp.float32)
    taps = taps_ref[...].astype(jnp.float32)
    first[...] = taps[:, :, :TILE].reshape(ROWS * BANDS, TILE)
    last[...] = jnp.broadcast_to(taps[:, :, TILE:], (ROWS, BANDS, TILE)).reshape(
        ROWS * BANDS, TILE
    )
    rows, lanes = row_ids((TILE, TILE)), lane_ids((TILE, TILE))
    in_first = lanes >= rows
    on_diag = lanes == rows
    low = lane_ids((ROWS, TILE)) < HALF
    after[:ROWS, :] = jnp.zeros((ROWS, TILE), jnp.float32)

    def write_block(block, before, here):
        out_buf[:, pl.ds(start(block, TILE), TILE)] = jnp.where(low, before, here)

    def one_band(band, before):
        for part in range(BAND_SLABS):
            slab = band * BAND_SLABS + part
            for inner in range(SLAB_BLOCKS):
                block = slab * SLAB_BLOCKS + inner
                value = data_ref[slab, :, inner * TILE : (inner + 1) * TILE].astype(jnp.float32)
                value = flags_ref[pl.ds(block, 1), :] * (value - sky[tiles_ref[slab, inner]])
                resid[pl.ds(start(block, ROWS), ROWS), :] = value
        for det in range(ROWS):
            pair = det * BANDS + band
            turned = circulant(first[pl.ds(pair, 1), :])
            end = jnp.broadcast_to(last[pl.ds(pair, 1), :], (TILE, TILE))
            upper = jnp.where(in_first, turned, 0.0)
            lower = jnp.where(in_first, jnp.where(on_diag, end, 0.0), turned)
            kernel = jnp.concatenate([upper, lower], axis=1).astype(jnp.bfloat16)
            base = band * BAND_BLOCKS * ROWS + det
            part = resid[pl.ds(base, BAND_BLOCKS, stride=ROWS), :].astype(jnp.bfloat16)
            spread = jnp.dot(part, kernel, preferred_element_type=jnp.float32)
            same[pl.ds(base, BAND_BLOCKS, stride=ROWS), :] = spread[:, :TILE]
            after[pl.ds(base + ROWS, BAND_BLOCKS, stride=ROWS), :] = spread[:, TILE:]
        for inner in range(BAND_BLOCKS):
            block = band * BAND_BLOCKS + inner
            place = pl.ds(start(block, ROWS), ROWS)
            here = pltpu.roll(same[place, :] + after[place, :], HALF, 1)
            if inner == 0:

                @pl.when(band > 0)
                def _():
                    write_block(block - 1, before, here)
                    out_copy(band - 1).start()

            else:
                write_block(block - 1, before, here)
            before = here
        return before

    before = lax.fori_loop(0, BANDS, one_band, jnp.zeros((ROWS, TILE), jnp.float32))
    write_block(BLOCKS - 1, before, pltpu.roll(after[BLOCKS * ROWS :, :], HALF, 1))
    out_copy(BANDS - 1).start()
    for band in range(BANDS):
        out_copy(band).wait()


def make_basis(positions, wafer_group):
    x_pos = positions[0]
    y_pos = positions[1]
    monomials = jnp.stack(
        [jnp.ones_like(x_pos), x_pos, y_pos, x_pos * x_pos, x_pos * y_pos, y_pos * y_pos]
    )
    member = (wafer_group[None, :] == jnp.arange(WAFERS, dtype=jnp.int32)[:, None]).astype(
        jnp.float32
    )
    basis_b = (member[:, None, :] * monomials[None]).reshape(WAFERS * POLY, -1).astype(jnp.bfloat16)
    basis_f = basis_b.astype(jnp.float32)
    gram_matrix = jnp.dot(basis_f, basis_f.T, precision=lax.Precision.HIGHEST)
    factor = jnp.linalg.cholesky(gram_matrix)
    lower_inv = lax.linalg.triangular_solve(
        factor, jnp.eye(WAFERS * POLY, dtype=jnp.float32), left_side=True, lower=True
    )
    inverse = jnp.dot(lower_inv.T, lower_inv, precision=lax.Precision.HIGHEST)
    return (basis_b, inverse)


def exchange(value, axis):
    size = lax.axis_size(axis)
    return [
        lax.ppermute(value, axis, [(src, (src + step) % size) for src in range(size)])
        for step in range(1, size)
    ]


def local(timestreams, filter_taps, scan_bounds, tile_index, det_weights, positions, wafer_group):
    f32, bf16 = jnp.float32, jnp.bfloat16
    shape = jax.ShapeDtypeStruct
    buffer = pltpu.VMEM
    quad = lax.axis_index("q")
    group = lax.axis_index("g")
    slab = lax.axis_index(SLAB_AXES)
    taps = filter_taps.reshape(ROWS, BANDS, TAPS)
    meta = jnp.pad(tile_index[0].astype(bf16), (0, TILE - SLAB_BLOCKS))
    filtered = call(
        forward_kernel,
        shape((SLABS, ROWS, SLAB_LEN + TILE), bf16),
        [hbm(), hbm(), vmem()],
        hbm(),
        [
            buffer((ROWS, SAMP), bf16),
            buffer((ROWS, BANDS, TAPS), bf16),
            buffer(((BLOCKS + 1) * ROWS, TILE), f32),
            buffer((BLOCKS * ROWS, TILE), f32),
            buffer((SLABS, ROWS, SLAB_LEN + TILE), bf16),
            buffer((ROWS * BANDS, TILE), f32),
            buffer((ROWS * BANDS, TILE), f32),
            pltpu.SemaphoreType.DMA((2, BANDS + 1)),
        ],
        limit=60,
        micros=7,
    )(timestreams, taps, jnp.broadcast_to(meta[None], (ROWS, TILE)))
    gathered = lax.all_to_all(filtered, SLAB_AXES, split_axis=0, concat_axis=0, tiled=True)

    basis, inverse = make_basis(positions, wafer_group)
    basis_t = jnp.concatenate([basis, basis], axis=0).T
    weights = det_weights[0].astype(f32)
    lane_weights = jnp.broadcast_to(weights[:, None], (DET, TILE))
    row_weights = jnp.sum(weights.reshape(DET // TILE, TILE), axis=0)
    own_rows = lax.dynamic_slice_in_dim(row_weights, group * ROWS + quad * SHARE, SHARE)
    own_rows = jnp.broadcast_to(jnp.tile(own_rows, 2)[:, None], (2 * SHARE, TILE))
    cleaned, sums, tiles = call(
        clean_kernel,
        (
            shape((SLABS, ROWS, SLAB_LEN), bf16),
            shape((SLABS, SLAB_BLOCKS * SHARE, TILE), f32),
            shape((SLABS, TILE), jnp.int32),
        ),
        [smem()] + [vmem()] * 5,
        (vmem(), vmem(), vmem()),
    )(scan_bounds - slab * SLAB_LEN, gathered, basis, basis_t, inverse, lane_weights)
    sums = lax.all_to_all(sums, SLAB_AXES, split_axis=0, concat_axis=0, tiled=True)
    flags, scans = call(
        scan_kernel,
        (shape((BLOCKS, TILE), f32), shape((TILES + 2 * SHARE, TILE), f32)),
        [smem(), smem(), vmem()],
        (vmem(), vmem()),
        [buffer((TILES, 8, TILE), f32)],
    )(scan_bounds, tiles, own_rows)
    cleaned, sums = lax.optimization_barrier((cleaned, sums))
    returned = lax.all_to_all(cleaned, SLAB_AXES, split_axis=0, concat_axis=0, tiled=True)

    part = call(
        bin_kernel,
        shape((SUM_ROWS + TILES + 2 * SHARE, TILE), f32),
        [smem(), vmem(), vmem()],
        vmem(),
        [buffer((TILES, 2 * SHARE, TILE), f32)],
    )(tiles, sums, scans)
    sky, sky_b = call(
        sky_kernel,
        (shape((SUM_ROWS, TILE), f32), shape((SUM_ROWS, TILE), bf16)),
        [vmem()] * OBS,
        (vmem(), vmem()),
        micros=1,
    )(part, *exchange(part, "obs"))
    held = jnp.stack([sky_b] + exchange(sky_b, "q")).reshape(QUADS, TILES, SHARE, TILE)
    held = [
        lax.dynamic_index_in_dim(held, lax.rem(quad - src + QUADS, QUADS), 0, keepdims=False)
        for src in range(QUADS)
    ]
    sky_rows = jnp.stack(held, axis=1).reshape(TILES, ROWS, TILE)
    sky_row = lax.dynamic_slice_in_dim(
        sky.reshape(TILES, SHARE, TILE), lax.axis_index("obs"), 1, 1
    )
    moves = [
        ((o * QUADS + q) * GROUPS + g, g * ROWS + q * SHARE + o)
        for o in range(OBS)
        for q in range(QUADS)
        for g in range(GROUPS)
    ]
    sky_own = lax.ppermute(sky_row, ALL_AXES, moves)
    out = call(
        adjoint_kernel,
        shape((1, ROWS, SAMP), f32),
        [smem(), vmem(), vmem(), vmem(), vmem()],
        hbm(),
        [
            buffer((TILES, ROWS, TILE), f32),
            buffer((BLOCKS * ROWS, TILE), f32),
            buffer((BLOCKS * ROWS, TILE), f32),
            buffer(((BLOCKS + 1) * ROWS, TILE), f32),
            buffer((ROWS, SAMP), f32),
            buffer((ROWS * BANDS, TILE), f32),
            buffer((ROWS * BANDS, TILE), f32),
            pltpu.SemaphoreType.DMA((BANDS,)),
        ],
        micros=9,
    )(tiles, flags, returned, sky_rows, taps)
    return (out, sky_own)


def solution(mesh):
    split = Mesh(mesh.devices.reshape(OBS, QUADS, GROUPS), ALL_AXES)
    placed = (
        P("obs", SLAB_AXES, None),
        P("obs", SLAB_AXES, None, None),
        P("obs", None),
        P("obs", SLAB_AXES),
        P("obs", None),
        P(),
        P(),
    )
    return jax.shard_map(
        local,
        mesh=split,
        in_specs=placed,
        out_specs=(P("obs", SLAB_AXES, None), P(None, ALL_AXES, None)),
        check_vma=False,
    )
```

```python
import functools

import jax
import jax.numpy as jnp
from jax import lax
from jax.experimental import pallas as pl
from jax.experimental.pallas import tpu as pltpu
from jax.sharding import Mesh
from jax.sharding import PartitionSpec as P

TAPS = 129
BANDS = 8
TILE = 128
WAFERS = 8
POLY = 6
NINT = 16
OBS = 4
DET = 512
SAMP = 32768
TILES = 16

QUADS = 4
GROUPS = 8
ROWS = 16
BLOCKS = SAMP // TILE
SLABS = QUADS * GROUPS
SLAB_BLOCKS = BLOCKS // SLABS
BAND_BLOCKS = BLOCKS // BANDS
HALF = TILE // 2
GROUP_AXES = ("obs", "q")
SLAB_AXES = ("q", "g")
ALL_AXES = ("obs", "q", "g")

prior_weight = 1.0
MIB = 1024 * 1024
BAND_SLABS = SLABS // BANDS
SLAB_LEN = SLAB_BLOCKS * TILE
SHARE = TILE // SLABS
SUM_ROWS = TILES * SHARE


def vmem():
    return pl.BlockSpec(memory_space=pltpu.VMEM)


def smem():
    return pl.BlockSpec(memory_space=pltpu.SMEM)


def hbm():
    return pl.BlockSpec(memory_space=pltpu.HBM)


def call(kernel, out_shape, in_specs, out_specs, scratch=(), limit=32, micros=2):
    return pl.pallas_call(
        kernel,
        out_shape=out_shape,
        in_specs=in_specs,
        out_specs=out_specs,
        scratch_shapes=list(scratch),
        compiler_params=pltpu.CompilerParams(vmem_limit_bytes=limit * MIB),
        cost_estimate=pl.CostEstimate(
            flops=0, bytes_accessed=micros * 3_000_000, transcendentals=0
        ),
    )


def lane_ids(shape):
    return lax.broadcasted_iota(jnp.int32, shape, len(shape) - 1)


def row_ids(shape):
    return lax.broadcasted_iota(jnp.int32, shape, len(shape) - 2)


def circulant(row):
    return pltpu.roll(jnp.broadcast_to(row, (TILE, TILE)), 0, 1, stride=1, stride_axis=0)


def start(block, size):
    return pl.multiple_of(block * size, size)


def forward_kernel(
    x_ref, taps_ref, tiles_ref, y_ref, x_buf, taps_buf, shifted, summed, y_buf, first, last, tiles, sems
):
    taps_copy = pltpu.make_async_copy(taps_ref, taps_buf, sems.at[0, BANDS])
    taps_copy.start()
    tiles_copy = pltpu.make_async_copy(tiles_ref, tiles, sems.at[1, BANDS])
    tiles_copy.start()

    def x_copy(band):
        part = pl.ds(start(band, BAND_BLOCKS * TILE), BAND_BLOCKS * TILE)
        return pltpu.make_async_copy(x_ref.at[0, :, part], x_buf.at[:, part], sems.at[0, band])

    def y_copy(band):
        part = pl.ds(band * BAND_SLABS, BAND_SLABS)
        return pltpu.make_async_copy(y_buf.at[part], y_ref.at[part], sems.at[1, band])

    for band in range(BANDS):
        x_copy(band).start()
    low = lane_ids((ROWS, TILE)) < HALF
    rows, lanes = row_ids((TILE, TILE)), lane_ids((TILE, TILE))
    in_first = lanes <= rows
    on_diag = lanes == rows
    reverse = (rows == ((TILE - lanes) & (TILE - 1))).astype(jnp.float32).astype(jnp.bfloat16)
    taps_copy.wait()
    taps = taps_buf[...].astype(jnp.float32)
    front = taps[:, :, :TILE].reshape(ROWS * BANDS, TILE).astype(jnp.bfloat16)
    first[...] = jnp.dot(front, reverse, preferred_element_type=jnp.float32)
    last[...] = jnp.broadcast_to(taps[:, :, TILE:], (ROWS, BANDS, TILE)).reshape(
        ROWS * BANDS, TILE
    )

    def rolled(block):
        part = x_buf[:, pl.ds(start(block, TILE), TILE)]
        return pltpu.roll(part.astype(jnp.float32), HALF, 1)

    tiles_copy.wait()
    lane = lane_ids((ROWS, TILE))
    meta = jnp.zeros((ROWS, TILE), jnp.int32)
    for block in range(SLAB_BLOCKS):
        meta = jnp.where(lane == block, tiles[0, block], meta)
    meta = meta.astype(jnp.float32).astype(jnp.bfloat16)
    x_copy(0).wait()
    opening = rolled(0)
    shifted[:ROWS, :] = jnp.where(low, 0.0, opening)

    def one_band(band, before):
        @pl.when(band < BANDS - 1)
        def _():
            x_copy(band + 1).wait()

        for inner in range(1, BAND_BLOCKS + 1):
            block = band * BAND_BLOCKS + inner
            if inner == BAND_BLOCKS:
                here = jnp.where(
                    band < BANDS - 1, rolled(jnp.minimum(block, BLOCKS - 1)), 0.0
                )
            else:
                here = rolled(block)
            shifted[pl.ds(start(block, ROWS), ROWS), :] = jnp.where(low, before, here)
            before = here
        for det in range(ROWS):
            pair = det * BANDS + band
            turned = circulant(first[pl.ds(pair, 1), :])
            end = jnp.broadcast_to(last[pl.ds(pair, 1), :], (TILE, TILE))
            upper = jnp.where(in_first, turned, 0.0)
            lower = jnp.where(in_first, jnp.where(on_diag, end, 0.0), turned)
            kernel = jnp.concatenate([upper, lower], axis=0).astype(jnp.bfloat16)
            base = band * BAND_BLOCKS * ROWS + det
            one = shifted[pl.ds(base, BAND_BLOCKS, stride=ROWS), :]
            two = shifted[pl.ds(base + ROWS, BAND_BLOCKS, stride=ROWS), :]
            window = jnp.concatenate([one, two], axis=1).astype(jnp.bfloat16)
            summed[pl.ds(base, BAND_BLOCKS, stride=ROWS), :] = jnp.dot(
                window, kernel, preferred_element_type=jnp.float32
            )
        for part in range(BAND_SLABS):
            slab = band * BAND_SLABS + part
            for inner in range(SLAB_BLOCKS):
                block = slab * SLAB_BLOCKS + inner
                y_buf[slab, :, inner * TILE : (inner + 1) * TILE] = summed[
                    pl.ds(start(block, ROWS), ROWS), :
                ].astype(jnp.bfloat16)
            y_buf[slab, :, SLAB_LEN:] = meta
        y_copy(band).start()
        return before

    lax.fori_loop(0, BANDS, one_band, opening)
    for band in range(BANDS):
        y_copy(band).wait()


def count_flags(bounds_ref, blocks, offset):
    sample = (row_ids((blocks, TILE)) + offset) * TILE + lane_ids((blocks, TILE))
    passed = jnp.zeros((blocks, TILE), jnp.int32)
    for bound in range(2 * NINT):
        passed = passed + (bounds_ref[0, bound] <= sample).astype(jnp.int32)
    return (passed & 1).astype(jnp.float32)


def clean_kernel(
    bounds_ref, data_ref, basis_ref, basis_t_ref, inverse_ref, weight_ref, out_ref, sums_ref, tiles_ref, sums
):
    data = data_ref[:, :, :SLAB_LEN].reshape(DET, SLAB_LEN)
    tiles_ref[...] = data_ref[:, :, SLAB_LEN:].astype(jnp.float32)[:, 0, :].astype(jnp.int32)
    raw = jnp.dot(basis_ref[...], data, preferred_element_type=jnp.float32)
    coef = jnp.dot(
        inverse_ref[...],
        raw,
        precision=lax.Precision.HIGHEST,
        preferred_element_type=jnp.float32,
    )
    high = coef.astype(jnp.bfloat16)
    rest = (coef - high.astype(jnp.float32)).astype(jnp.bfloat16)
    both = jnp.concatenate([high, rest], axis=0)
    fitted = jnp.dot(basis_t_ref[...], both, preferred_element_type=jnp.float32)
    cleaned = (data.astype(jnp.float32) - fitted).astype(jnp.bfloat16)
    out_ref[...] = cleaned.reshape(out_ref.shape)
    flags = count_flags(bounds_ref, SLAB_BLOCKS, 0)
    for block in range(SLAB_BLOCKS):
        part = cleaned[:, block * TILE : (block + 1) * TILE].astype(jnp.float32)
        weighted = (part * weight_ref[...]).reshape(DET // TILE, TILE, TILE)
        total = jnp.sum(weighted, axis=0) * flags[block : block + 1, :]
        for quad in range(QUADS):
            for group in range(GROUPS):
                row = group * ROWS + quad * SHARE
                sums[quad * GROUPS + group, block * SHARE : (block + 1) * SHARE, :] = total[
                    row : row + SHARE, :
                ]
    sums_ref[...] = sums[...].astype(jnp.bfloat16)


def scan_kernel(bounds_ref, tiles_ref, weight_ref, flags_ref, scan_ref, acc):
    for band in range(BANDS):
        flags_ref[band * BAND_BLOCKS : (band + 1) * BAND_BLOCKS, :] = count_flags(
            bounds_ref, BAND_BLOCKS, band * BAND_BLOCKS
        )
    acc[...] = jnp.zeros_like(acc)

    def add_slab(slab, carry):
        for inner in range(SLAB_BLOCKS):
            tile = tiles_ref[slab, inner]
            row = flags_ref[pl.ds(slab * SLAB_BLOCKS + inner, 1), :]
            acc[tile] = acc[tile] + jnp.broadcast_to(row, (8, TILE))
        return carry

    lax.fori_loop(0, SLABS, add_slab, 0)
    for tile in range(TILES):
        scan_ref[tile : tile + 1, :] = acc[tile, :1, :]
    scan_ref[TILES:, :] = weight_ref[...]


def bin_kernel(tiles_ref, sums_ref, scan_ref, out_ref, acc):
    acc[...] = jnp.zeros_like(acc)
    upper = row_ids((2 * SHARE, TILE)) < SHARE

    def add_slab(slab, carry):
        received = sums_ref[slab].astype(jnp.float32)
        for pair in range(SLAB_BLOCKS // 2):
            part = received[pair * 2 * SHARE : (pair + 1) * 2 * SHARE, :]
            even = tiles_ref[slab, 2 * pair]
            acc[even] = acc[even] + jnp.where(upper, part, 0.0)
            odd = tiles_ref[slab, 2 * pair + 1]
            acc[odd] = acc[odd] + jnp.where(upper, 0.0, part)
        return carry

    lax.fori_loop(0, SLABS, add_slab, 0)
    for tile in range(TILES):
        both = acc[tile]
        out_ref[tile * SHARE : (tile + 1) * SHARE, :] = both[:SHARE, :] + both[SHARE:, :]
    out_ref[SUM_ROWS:, :] = scan_ref[...]


def sky_kernel(a_ref, b_ref, c_ref, d_ref, sky_ref, sky_b_ref):
    refs = (a_ref, b_ref, c_ref, d_ref)
    upper = row_ids((2 * SHARE, TILE)) < SHARE
    weights = [ref[SUM_ROWS + TILES :, :] for ref in refs]
    for pair in range(TILES // 2):
        rows = slice(pair * 2 * SHARE, (pair + 1) * 2 * SHARE)
        total = jnp.zeros((2 * SHARE, TILE), jnp.float32)
        hits = jnp.zeros((2 * SHARE, TILE), jnp.float32)
        for ref, weight in zip(refs, weights):
            total = total + ref[rows, :]
            even = ref[SUM_ROWS + 2 * pair : SUM_ROWS + 2 * pair + 1, :]
            odd = ref[SUM_ROWS + 2 * pair + 1 : SUM_ROWS + 2 * pair + 2, :]
            hits = hits + weight * jnp.where(upper, even, odd)
        sky_ref[rows, :] = total / (hits + prior_weight)
    sky_b_ref[...] = sky_ref[...].astype(jnp.bfloat16)


def adjoint_kernel(
    tiles_ref, flags_ref, data_ref, sky_ref, taps_ref, out_ref, sky, resid, same, after, out_buf, first, last, sems
):
    def out_copy(band):
        part = pl.ds(start(band, BAND_BLOCKS * TILE), BAND_BLOCKS * TILE)
        return pltpu.make_async_copy(out_buf.at[:, part], out_ref.at[0, :, part], sems.at[band])

    sky[...] = sky_ref[...].astype(jnp.float32)
    taps = taps_ref[...].astype(jnp.float32)
    first[...] = taps[:, :, :TILE].reshape(ROWS * BANDS, TILE)
    last[...] = jnp.broadcast_to(taps[:, :, TILE:], (ROWS, BANDS, TILE)).reshape(
        ROWS * BANDS, TILE
    )
    rows, lanes = row_ids((TILE, TILE)), lane_ids((TILE, TILE))
    in_first = lanes >= rows
    on_diag = lanes == rows
    low = lane_ids((ROWS, TILE)) < HALF
    after[:ROWS, :] = jnp.zeros((ROWS, TILE), jnp.float32)

    def write_block(block, before, here):
        out_buf[:, pl.ds(start(block, TILE), TILE)] = jnp.where(low, before, here)

    def one_band(band, before):
        for part in range(BAND_SLABS):
            slab = band * BAND_SLABS + part
            for inner in range(SLAB_BLOCKS):
                block = slab * SLAB_BLOCKS + inner
                value = data_ref[slab, :, inner * TILE : (inner + 1) * TILE].astype(jnp.float32)
                value = flags_ref[pl.ds(block, 1), :] * (value - sky[tiles_ref[slab, inner]])
                resid[pl.ds(start(block, ROWS), ROWS), :] = value
        for det in range(ROWS):
            pair = det * BANDS + band
            turned = circulant(first[pl.ds(pair, 1), :])
            end = jnp.broadcast_to(last[pl.ds(pair, 1), :], (TILE, TILE))
            upper = jnp.where(in_first, turned, 0.0)
            lower = jnp.where(in_first, jnp.where(on_diag, end, 0.0), turned)
            kernel = jnp.concatenate([upper, lower], axis=1).astype(jnp.bfloat16)
            base = band * BAND_BLOCKS * ROWS + det
            part = resid[pl.ds(base, BAND_BLOCKS, stride=ROWS), :].astype(jnp.bfloat16)
            spread = jnp.dot(part, kernel, preferred_element_type=jnp.float32)
            same[pl.ds(base, BAND_BLOCKS, stride=ROWS), :] = spread[:, :TILE]
            after[pl.ds(base + ROWS, BAND_BLOCKS, stride=ROWS), :] = spread[:, TILE:]
        for inner in range(BAND_BLOCKS):
            block = band * BAND_BLOCKS + inner
            place = pl.ds(start(block, ROWS), ROWS)
            here = pltpu.roll(same[place, :] + after[place, :], HALF, 1)
            if inner == 0:

                @pl.when(band > 0)
                def _():
                    write_block(block - 1, before, here)
                    out_copy(band - 1).start()

            else:
                write_block(block - 1, before, here)
            before = here
        return before

    before = lax.fori_loop(0, BANDS, one_band, jnp.zeros((ROWS, TILE), jnp.float32))
    write_block(BLOCKS - 1, before, pltpu.roll(after[BLOCKS * ROWS :, :], HALF, 1))
    out_copy(BANDS - 1).start()
    for band in range(BANDS):
        out_copy(band).wait()


def make_basis(positions, wafer_group):
    x_pos = positions[0]
    y_pos = positions[1]
    monomials = jnp.stack(
        [jnp.ones_like(x_pos), x_pos, y_pos, x_pos * x_pos, x_pos * y_pos, y_pos * y_pos]
    )
    member = (wafer_group[None, :] == jnp.arange(WAFERS, dtype=jnp.int32)[:, None]).astype(
        jnp.float32
    )
    basis_b = (member[:, None, :] * monomials[None]).reshape(WAFERS * POLY, -1).astype(jnp.bfloat16)
    basis_f = basis_b.astype(jnp.float32)
    gram_matrix = jnp.dot(basis_f, basis_f.T, precision=lax.Precision.HIGHEST)
    factor = jnp.linalg.cholesky(gram_matrix)
    lower_inv = lax.linalg.triangular_solve(
        factor, jnp.eye(WAFERS * POLY, dtype=jnp.float32), left_side=True, lower=True
    )
    inverse = jnp.dot(lower_inv.T, lower_inv, precision=lax.Precision.HIGHEST)
    return (basis_b, inverse)


def exchange(value, axis):
    size = lax.axis_size(axis)
    return [
        lax.ppermute(value, axis, [(src, (src + step) % size) for src in range(size)])
        for step in range(1, size)
    ]


def local(timestreams, filter_taps, scan_bounds, tile_index, det_weights, positions, wafer_group):
    f32, bf16 = jnp.float32, jnp.bfloat16
    shape = jax.ShapeDtypeStruct
    buffer = pltpu.VMEM
    quad = lax.axis_index("q")
    group = lax.axis_index("g")
    slab = lax.axis_index(SLAB_AXES)
    taps = filter_taps.reshape(ROWS, BANDS, TAPS)
    filtered = call(
        forward_kernel,
        shape((SLABS, ROWS, SLAB_LEN + TILE), bf16),
        [hbm(), hbm(), hbm()],
        hbm(),
        [
            buffer((ROWS, SAMP), bf16),
            buffer((ROWS, BANDS, TAPS), bf16),
            buffer(((BLOCKS + 1) * ROWS, TILE), f32),
            buffer((BLOCKS * ROWS, TILE), f32),
            buffer((SLABS, ROWS, SLAB_LEN + TILE), bf16),
            buffer((ROWS * BANDS, TILE), f32),
            buffer((ROWS * BANDS, TILE), f32),
            pltpu.SMEM((1, SLAB_BLOCKS), jnp.int32),
            pltpu.SemaphoreType.DMA((2, BANDS + 1)),
        ],
        limit=60,
        micros=7,
    )(timestreams, taps, tile_index)
    gathered = lax.all_to_all(filtered, SLAB_AXES, split_axis=0, concat_axis=0, tiled=True)

    basis, inverse = make_basis(positions, wafer_group)
    basis_t = jnp.concatenate([basis, basis], axis=0).T
    weights = det_weights[0].astype(f32)
    lane_weights = jnp.broadcast_to(weights[:, None], (DET, TILE))
    row_weights = jnp.sum(weights.reshape(DET // TILE, TILE), axis=0)
    own_rows = lax.dynamic_slice_in_dim(row_weights, group * ROWS + quad * SHARE, SHARE)
    own_rows = jnp.broadcast_to(jnp.tile(own_rows, 2)[:, None], (2 * SHARE, TILE))
    cleaned, sums, tiles = call(
        clean_kernel,
        (
            shape((SLABS, ROWS, SLAB_LEN), bf16),
            shape((SLABS, SLAB_BLOCKS * SHARE, TILE), bf16),
            shape((SLABS, TILE), jnp.int32),
        ),
        [smem()] + [vmem()] * 5,
        (vmem(), vmem(), vmem()),
        [buffer((SLABS, SLAB_BLOCKS * SHARE, TILE), f32)],
    )(scan_bounds - slab * SLAB_LEN, gathered, basis, basis_t, inverse, lane_weights)
    sums = lax.all_to_all(sums, SLAB_AXES, split_axis=0, concat_axis=0, tiled=True)
    flags, scans = call(
        scan_kernel,
        (shape((BLOCKS, TILE), f32), shape((TILES + 2 * SHARE, TILE), f32)),
        [smem(), smem(), vmem()],
        (vmem(), vmem()),
        [buffer((TILES, 8, TILE), f32)],
    )(scan_bounds, tiles, own_rows)
    cleaned, sums, flags, scans = lax.optimization_barrier((cleaned, sums, flags, scans))
    returned = lax.all_to_all(cleaned, SLAB_AXES, split_axis=0, concat_axis=0, tiled=True)

    part = call(
        bin_kernel,
        shape((SUM_ROWS + TILES + 2 * SHARE, TILE), f32),
        [smem(), vmem(), vmem()],
        vmem(),
        [buffer((TILES, 2 * SHARE, TILE), f32)],
    )(tiles, sums, scans)
    sky, sky_b = call(
        sky_kernel,
        (shape((SUM_ROWS, TILE), f32), shape((SUM_ROWS, TILE), bf16)),
        [vmem()] * OBS,
        (vmem(), vmem()),
        micros=1,
    )(part, *exchange(part, "obs"))
    held = jnp.stack([sky_b] + exchange(sky_b, "q")).reshape(QUADS, TILES, SHARE, TILE)
    held = [
        lax.dynamic_index_in_dim(held, lax.rem(quad - src + QUADS, QUADS), 0, keepdims=False)
        for src in range(QUADS)
    ]
    sky_rows = jnp.stack(held, axis=1).reshape(TILES, ROWS, TILE)
    sky_row = lax.dynamic_slice_in_dim(
        sky.reshape(TILES, SHARE, TILE), lax.axis_index("obs"), 1, 1
    )
    moves = [
        ((o * QUADS + q) * GROUPS + g, g * ROWS + q * SHARE + o)
        for o in range(OBS)
        for q in range(QUADS)
        for g in range(GROUPS)
    ]
    sky_row, returned = lax.optimization_barrier((sky_row, returned))
    sky_own = lax.ppermute(sky_row, ALL_AXES, moves)
    out = call(
        adjoint_kernel,
        shape((1, ROWS, SAMP), f32),
        [smem(), vmem(), vmem(), vmem(), vmem()],
        hbm(),
        [
            buffer((TILES, ROWS, TILE), f32),
            buffer((BLOCKS * ROWS, TILE), f32),
            buffer((BLOCKS * ROWS, TILE), f32),
            buffer(((BLOCKS + 1) * ROWS, TILE), f32),
            buffer((ROWS, SAMP), f32),
            buffer((ROWS * BANDS, TILE), f32),
            buffer((ROWS * BANDS, TILE), f32),
            pltpu.SemaphoreType.DMA((BANDS,)),
        ],
        micros=9,
    )(tiles, flags, returned, sky_rows, taps)
    return (out, sky_own)


def solution(mesh):
    split = Mesh(mesh.devices.reshape(OBS, QUADS, GROUPS), ALL_AXES)
    placed = (
        P("obs", SLAB_AXES, None),
        P("obs", SLAB_AXES, None, None),
        P("obs", None),
        P("obs", SLAB_AXES),
        P("obs", None),
        P(),
        P(),
    )
    return jax.shard_map(
        local,
        mesh=split,
        in_specs=placed,
        out_specs=(P("obs", SLAB_AXES, None), P(None, ALL_AXES, None)),
        check_vma=False,
    )
```

```python
import functools

import jax
import jax.numpy as jnp
from jax import lax
from jax.experimental import pallas as pl
from jax.experimental.pallas import tpu as pltpu
from jax.sharding import Mesh
from jax.sharding import PartitionSpec as P

TAPS = 129
BANDS = 8
TILE = 128
WAFERS = 8
POLY = 6
NINT = 16
OBS = 4
DET = 512
SAMP = 32768
TILES = 16

QUADS = 4
GROUPS = 8
ROWS = 16
BLOCKS = SAMP // TILE
SLABS = QUADS * GROUPS
SLAB_BLOCKS = BLOCKS // SLABS
BAND_BLOCKS = BLOCKS // BANDS
HALF = TILE // 2
GROUP_AXES = ("obs", "q")
SLAB_AXES = ("q", "g")
ALL_AXES = ("obs", "q", "g")

prior_weight = 1.0
MIB = 1024 * 1024
BAND_SLABS = SLABS // BANDS
SLAB_LEN = SLAB_BLOCKS * TILE
SHARE = TILE // SLABS
SUM_ROWS = TILES * SHARE


def vmem():
    return pl.BlockSpec(memory_space=pltpu.VMEM)


def smem():
    return pl.BlockSpec(memory_space=pltpu.SMEM)


def hbm():
    return pl.BlockSpec(memory_space=pltpu.HBM)


def call(kernel, out_shape, in_specs, out_specs, scratch=(), limit=32, micros=2):
    return pl.pallas_call(
        kernel,
        out_shape=out_shape,
        in_specs=in_specs,
        out_specs=out_specs,
        scratch_shapes=list(scratch),
        compiler_params=pltpu.CompilerParams(vmem_limit_bytes=limit * MIB),
        cost_estimate=pl.CostEstimate(
            flops=0, bytes_accessed=micros * 3_000_000, transcendentals=0
        ),
    )


def share_of(quad, group):
    turn = (quad - 2 * (group & 1)) & 3
    near = turn >> 1
    return ((turn + 1) & 2) | (((group >> 2) ^ 1) ^ near), near


def quad_of(share, group):
    near = (share & 1) ^ ((group >> 2) ^ 1)
    return (2 * near + (near ^ (share >> 1)) + 2 * (group & 1)) & 3


def sent_row(obs, quad, group):
    step = (obs - (group >> 1)) & 3
    near = share_of(quad, group)[1]
    code = near * ((2 - step) & 3) + (1 - near) * (step ^ (step >> 1))
    return code ^ (2 * ((group >> 1) & 1))


def lane_ids(shape):
    return lax.broadcasted_iota(jnp.int32, shape, len(shape) - 1)


def row_ids(shape):
    return lax.broadcasted_iota(jnp.int32, shape, len(shape) - 2)


def circulant(row):
    return pltpu.roll(jnp.broadcast_to(row, (TILE, TILE)), 0, 1, stride=1, stride_axis=0)


def start(block, size):
    return pl.multiple_of(block * size, size)


def forward_kernel(
    x_ref, taps_ref, tiles_ref, y_ref, x_buf, taps_buf, shifted, summed, y_buf, first, last, tiles, sems
):
    taps_copy = pltpu.make_async_copy(taps_ref, taps_buf, sems.at[0, BANDS])
    taps_copy.start()
    tiles_copy = pltpu.make_async_copy(tiles_ref, tiles, sems.at[1, BANDS])
    tiles_copy.start()

    def x_copy(band):
        part = pl.ds(start(band, BAND_BLOCKS * TILE), BAND_BLOCKS * TILE)
        return pltpu.make_async_copy(x_ref.at[0, :, part], x_buf.at[:, part], sems.at[0, band])

    def y_copy(band):
        part = pl.ds(band * BAND_SLABS, BAND_SLABS)
        return pltpu.make_async_copy(y_buf.at[part], y_ref.at[part], sems.at[1, band])

    for band in range(BANDS):
        x_copy(band).start()
    low = lane_ids((ROWS, TILE)) < HALF
    rows, lanes = row_ids((TILE, TILE)), lane_ids((TILE, TILE))
    in_first = lanes <= rows
    on_diag = lanes == rows
    reverse = (rows == ((TILE - lanes) & (TILE - 1))).astype(jnp.float32).astype(jnp.bfloat16)
    taps_copy.wait()
    taps = taps_buf[...].astype(jnp.float32)
    front = taps[:, :, :TILE].reshape(ROWS * BANDS, TILE).astype(jnp.bfloat16)
    first[...] = jnp.dot(front, reverse, preferred_element_type=jnp.float32)
    last[...] = jnp.broadcast_to(taps[:, :, TILE:], (ROWS, BANDS, TILE)).reshape(
        ROWS * BANDS, TILE
    )

    def rolled(block):
        part = x_buf[:, pl.ds(start(block, TILE), TILE)]
        return pltpu.roll(part.astype(jnp.float32), HALF, 1)

    tiles_copy.wait()
    lane = lane_ids((ROWS, TILE))
    meta = jnp.zeros((ROWS, TILE), jnp.int32)
    for block in range(SLAB_BLOCKS):
        meta = jnp.where(lane == block, tiles[0, block], meta)
    meta = meta.astype(jnp.float32).astype(jnp.bfloat16)
    x_copy(0).wait()
    opening = rolled(0)
    shifted[:ROWS, :] = jnp.where(low, 0.0, opening)

    def one_band(band, before):
        @pl.when(band < BANDS - 1)
        def _():
            x_copy(band + 1).wait()

        for inner in range(1, BAND_BLOCKS + 1):
            block = band * BAND_BLOCKS + inner
            if inner == BAND_BLOCKS:
                here = jnp.where(
                    band < BANDS - 1, rolled(jnp.minimum(block, BLOCKS - 1)), 0.0
                )
            else:
                here = rolled(block)
            shifted[pl.ds(start(block, ROWS), ROWS), :] = jnp.where(low, before, here)
            before = here
        for det in range(ROWS):
            pair = det * BANDS + band
            turned = circulant(first[pl.ds(pair, 1), :])
            end = jnp.broadcast_to(last[pl.ds(pair, 1), :], (TILE, TILE))
            upper = jnp.where(in_first, turned, 0.0)
            lower = jnp.where(in_first, jnp.where(on_diag, end, 0.0), turned)
            kernel = jnp.concatenate([upper, lower], axis=0).astype(jnp.bfloat16)
            base = band * BAND_BLOCKS * ROWS + det
            one = shifted[pl.ds(base, BAND_BLOCKS, stride=ROWS), :]
            two = shifted[pl.ds(base + ROWS, BAND_BLOCKS, stride=ROWS), :]
            window = jnp.concatenate([one, two], axis=1).astype(jnp.bfloat16)
            summed[pl.ds(base, BAND_BLOCKS, stride=ROWS), :] = jnp.dot(
                window, kernel, preferred_element_type=jnp.float32
            )
        for part in range(BAND_SLABS):
            slab = band * BAND_SLABS + part
            for inner in range(SLAB_BLOCKS):
                block = slab * SLAB_BLOCKS + inner
                y_buf[slab, :, inner * TILE : (inner + 1) * TILE] = summed[
                    pl.ds(start(block, ROWS), ROWS), :
                ].astype(jnp.bfloat16)
            y_buf[slab, :, SLAB_LEN:] = meta
        y_copy(band).start()
        return before

    lax.fori_loop(0, BANDS, one_band, opening)
    for band in range(BANDS):
        y_copy(band).wait()


def count_flags(bounds_ref, blocks, offset):
    sample = (row_ids((blocks, TILE)) + offset) * TILE + lane_ids((blocks, TILE))
    passed = jnp.zeros((blocks, TILE), jnp.int32)
    for bound in range(2 * NINT):
        passed = passed + (bounds_ref[0, bound] <= sample).astype(jnp.int32)
    return (passed & 1).astype(jnp.float32)


def clean_kernel(
    bounds_ref, data_ref, basis_ref, basis_t_ref, inverse_ref, weight_ref, out_ref, sums_ref, tiles_ref, sums
):
    data = data_ref[:, :, :SLAB_LEN].reshape(DET, SLAB_LEN)
    tiles_ref[...] = data_ref[:, :, SLAB_LEN:].astype(jnp.float32)[:, 0, :].astype(jnp.int32)
    raw = jnp.dot(basis_ref[...], data, preferred_element_type=jnp.float32)
    coef = jnp.dot(
        inverse_ref[...],
        raw,
        precision=lax.Precision.HIGHEST,
        preferred_element_type=jnp.float32,
    )
    high = coef.astype(jnp.bfloat16)
    rest = (coef - high.astype(jnp.float32)).astype(jnp.bfloat16)
    both = jnp.concatenate([high, rest], axis=0)
    fitted = jnp.dot(basis_t_ref[...], both, preferred_element_type=jnp.float32)
    cleaned = (data.astype(jnp.float32) - fitted).astype(jnp.bfloat16)
    out_ref[...] = cleaned.reshape(out_ref.shape)
    flags = count_flags(bounds_ref, SLAB_BLOCKS, 0)
    for block in range(SLAB_BLOCKS):
        part = cleaned[:, block * TILE : (block + 1) * TILE].astype(jnp.float32)
        weighted = (part * weight_ref[...]).reshape(DET // TILE, TILE, TILE)
        total = jnp.sum(weighted, axis=0) * flags[block : block + 1, :]
        for quad in range(QUADS):
            for group in range(GROUPS):
                row = group * ROWS + share_of(quad, group)[0] * SHARE
                sums[quad * GROUPS + group, block * SHARE : (block + 1) * SHARE, :] = total[
                    row : row + SHARE, :
                ]
    sums_ref[...] = sums[...].astype(jnp.bfloat16)


def scan_kernel(bounds_ref, tiles_ref, weight_ref, flags_ref, scan_ref, acc):
    for band in range(BANDS):
        flags_ref[band * BAND_BLOCKS : (band + 1) * BAND_BLOCKS, :] = count_flags(
            bounds_ref, BAND_BLOCKS, band * BAND_BLOCKS
        )
    acc[...] = jnp.zeros_like(acc)

    def add_slab(slab, carry):
        for inner in range(SLAB_BLOCKS):
            tile = tiles_ref[slab, inner]
            row = flags_ref[pl.ds(slab * SLAB_BLOCKS + inner, 1), :]
            acc[tile] = acc[tile] + jnp.broadcast_to(row, (8, TILE))
        return carry

    lax.fori_loop(0, SLABS, add_slab, 0)
    for tile in range(TILES):
        scan_ref[tile : tile + 1, :] = acc[tile, :1, :]
    scan_ref[TILES:, :] = weight_ref[...]


def bin_kernel(tiles_ref, sums_ref, scan_ref, out_ref, *accs):
    for acc in accs:
        acc[...] = jnp.zeros_like(acc)
    upper = row_ids((2 * SHARE, TILE)) < SHARE

    def add_slabs(step, carry):
        for inner in range(SLAB_BLOCKS):
            pair = slice(inner // 2 * 2 * SHARE, (inner // 2 + 1) * 2 * SHARE)
            for which, acc in enumerate(accs):
                slab = step * len(accs) + which
                part = sums_ref[slab].astype(jnp.float32)[pair, :]
                part = jnp.where(upper, 0.0, part) if inner % 2 else jnp.where(upper, part, 0.0)
                tile = tiles_ref[slab, inner]
                acc[tile] = acc[tile] + part
        return carry

    lax.fori_loop(0, SLABS // len(accs), add_slabs, 0)
    for tile in range(TILES):
        both = sum(acc[tile] for acc in accs)
        out_ref[tile * SHARE : (tile + 1) * SHARE, :] = both[:SHARE, :] + both[SHARE:, :]
    out_ref[SUM_ROWS:, :] = scan_ref[...]


def sky_kernel(a_ref, b_ref, c_ref, d_ref, sky_ref, sky_b_ref):
    refs = (a_ref, b_ref, c_ref, d_ref)
    upper = row_ids((2 * SHARE, TILE)) < SHARE
    weights = [ref[SUM_ROWS + TILES :, :] for ref in refs]
    for pair in range(TILES // 2):
        rows = slice(pair * 2 * SHARE, (pair + 1) * 2 * SHARE)
        total = jnp.zeros((2 * SHARE, TILE), jnp.float32)
        hits = jnp.zeros((2 * SHARE, TILE), jnp.float32)
        for ref, weight in zip(refs, weights):
            total = total + ref[rows, :]
            even = ref[SUM_ROWS + 2 * pair : SUM_ROWS + 2 * pair + 1, :]
            odd = ref[SUM_ROWS + 2 * pair + 1 : SUM_ROWS + 2 * pair + 2, :]
            hits = hits + weight * jnp.where(upper, even, odd)
        sky_ref[rows, :] = total / (hits + prior_weight)
    sky_b_ref[...] = sky_ref[...].astype(jnp.bfloat16)


def adjoint_kernel(
    tiles_ref,
    flags_ref,
    data_ref,
    sky_ref,
    taps_ref,
    out_ref,
    sky,
    resid_a,
    resid_b,
    same_a,
    same_b,
    after_a,
    after_b,
    out_buf,
    first,
    last,
    sems,
):
    resid, same, after = (resid_a, resid_b), (same_a, same_b), (after_a, after_b)

    def out_copy(band):
        part = pl.ds(band * BAND_BLOCKS * TILE, BAND_BLOCKS * TILE)
        return pltpu.make_async_copy(out_buf.at[:, part], out_ref.at[0, :, part], sems.at[band])

    sky[...] = sky_ref[...].astype(jnp.float32)
    taps = taps_ref[...].astype(jnp.float32)
    first[...] = taps[:, :, :TILE].reshape(ROWS * BANDS, TILE)
    last[...] = jnp.broadcast_to(taps[:, :, TILE:], (ROWS, BANDS, TILE)).reshape(
        ROWS * BANDS, TILE
    )
    rows, lanes = row_ids((TILE, TILE)), lane_ids((TILE, TILE))
    in_first = lanes >= rows
    on_diag = lanes == rows
    low = lane_ids((ROWS, TILE)) < HALF
    zero = jnp.zeros((ROWS, TILE), jnp.float32)

    def make_residual(band, index):
        block = band * BAND_BLOCKS + index
        slab, inner = block // SLAB_BLOCKS, block % SLAB_BLOCKS
        value = data_ref[slab, :, inner * TILE : (inner + 1) * TILE].astype(jnp.float32)
        value = flags_ref[block : block + 1, :] * (value - sky[tiles_ref[slab, inner]])
        resid[band % 2][index * ROWS : (index + 1) * ROWS, :] = value

    def write_block(block, before, here):
        if block >= 0:
            out_buf[:, block * TILE : (block + 1) * TILE] = jnp.where(low, before, here)

    def join(band, index, before, spill):
        place = slice(index * ROWS, (index + 1) * ROWS)
        if index > 0:
            spill = after[band % 2][(index - 1) * ROWS : index * ROWS, :]
        here = pltpu.roll(same[band % 2][place, :] + spill, HALF, 1)
        write_block(band * BAND_BLOCKS + index - 1, before, here)
        return here

    for index in range(BAND_BLOCKS):
        make_residual(0, index)
    before, spill, next_spill = zero, zero, zero
    for band in range(BANDS + 1):
        if band >= 2:
            spill = next_spill
        if 1 <= band < BANDS:
            next_spill = after[(band - 1) % 2][(BAND_BLOCKS - 1) * ROWS :, :]
        for det in range(ROWS):
            if band < BANDS:
                pair = det * BANDS + band
                turned = circulant(first[pair : pair + 1, :])
                end = jnp.broadcast_to(last[pair : pair + 1, :], (TILE, TILE))
                upper = jnp.where(in_first, turned, 0.0)
                lower = jnp.where(in_first, jnp.where(on_diag, end, 0.0), turned)
                kernel = jnp.concatenate([upper, lower], axis=1).astype(jnp.bfloat16)
                part = resid[band % 2][pl.ds(det, BAND_BLOCKS, stride=ROWS), :]
                spread = jnp.dot(
                    part.astype(jnp.bfloat16), kernel, preferred_element_type=jnp.float32
                )
                same[band % 2][pl.ds(det, BAND_BLOCKS, stride=ROWS), :] = spread[:, :TILE]
                after[band % 2][pl.ds(det, BAND_BLOCKS, stride=ROWS), :] = spread[:, TILE:]
            for index in (2 * det, 2 * det + 1):
                if band + 1 < BANDS:
                    make_residual(band + 1, index)
                if band > 0:
                    before = join(band - 1, index, before, spill)
        if band >= 2:
            out_copy(band - 2).start()
    final = after[(BANDS - 1) % 2][(BAND_BLOCKS - 1) * ROWS :, :]
    write_block(BLOCKS - 1, before, pltpu.roll(final, HALF, 1))
    out_copy(BANDS - 1).start()
    for band in range(BANDS):
        out_copy(band).wait()


def make_basis(positions, wafer_group):
    x_pos = positions[0]
    y_pos = positions[1]
    monomials = jnp.stack(
        [jnp.ones_like(x_pos), x_pos, y_pos, x_pos * x_pos, x_pos * y_pos, y_pos * y_pos]
    )
    member = (wafer_group[None, :] == jnp.arange(WAFERS, dtype=jnp.int32)[:, None]).astype(
        jnp.float32
    )
    basis_b = (member[:, None, :] * monomials[None]).reshape(WAFERS * POLY, -1).astype(jnp.bfloat16)
    basis_f = basis_b.astype(jnp.float32)
    gram_matrix = jnp.dot(basis_f, basis_f.T, precision=lax.Precision.HIGHEST)
    factor = jnp.linalg.cholesky(gram_matrix)
    lower_inv = lax.linalg.triangular_solve(
        factor, jnp.eye(WAFERS * POLY, dtype=jnp.float32), left_side=True, lower=True
    )
    inverse = jnp.dot(lower_inv.T, lower_inv, precision=lax.Precision.HIGHEST)
    return (basis_b, inverse)


def exchange(value, axis):
    size = lax.axis_size(axis)
    return [
        lax.ppermute(value, axis, [(src, (src + step) % size) for src in range(size)])
        for step in range(1, size)
    ]


def local(timestreams, filter_taps, scan_bounds, tile_index, det_weights, positions, wafer_group):
    f32, bf16 = jnp.float32, jnp.bfloat16
    shape = jax.ShapeDtypeStruct
    buffer = pltpu.VMEM
    quad = lax.axis_index("q")
    group = lax.axis_index("g")
    slab = lax.axis_index(SLAB_AXES)
    taps = filter_taps.reshape(ROWS, BANDS, TAPS)
    filtered = call(
        forward_kernel,
        shape((SLABS, ROWS, SLAB_LEN + TILE), bf16),
        [hbm(), hbm(), hbm()],
        hbm(),
        [
            buffer((ROWS, SAMP), bf16),
            buffer((ROWS, BANDS, TAPS), bf16),
            buffer(((BLOCKS + 1) * ROWS, TILE), f32),
            buffer((BLOCKS * ROWS, TILE), f32),
            buffer((SLABS, ROWS, SLAB_LEN + TILE), bf16),
            buffer((ROWS * BANDS, TILE), f32),
            buffer((ROWS * BANDS, TILE), f32),
            pltpu.SMEM((1, SLAB_BLOCKS), jnp.int32),
            pltpu.SemaphoreType.DMA((2, BANDS + 1)),
        ],
        limit=60,
        micros=7,
    )(timestreams, taps, tile_index)
    gathered = lax.all_to_all(filtered, SLAB_AXES, split_axis=0, concat_axis=0, tiled=True)

    basis, inverse = make_basis(positions, wafer_group)
    basis_t = jnp.concatenate([basis, basis], axis=0).T
    weights = det_weights[0].astype(f32)
    lane_weights = jnp.broadcast_to(weights[:, None], (DET, TILE))
    row_weights = jnp.sum(weights.reshape(DET // TILE, TILE), axis=0)
    own_rows = lax.dynamic_slice_in_dim(row_weights, group * ROWS + share_of(quad, group)[0] * SHARE, SHARE)
    own_rows = jnp.broadcast_to(jnp.tile(own_rows, 2)[:, None], (2 * SHARE, TILE))
    cleaned, sums, tiles = call(
        clean_kernel,
        (
            shape((SLABS, ROWS, SLAB_LEN), bf16),
            shape((SLABS, SLAB_BLOCKS * SHARE, TILE), bf16),
            shape((SLABS, TILE), jnp.int32),
        ),
        [smem()] + [vmem()] * 5,
        (vmem(), vmem(), vmem()),
        [buffer((SLABS, SLAB_BLOCKS * SHARE, TILE), f32)],
    )(scan_bounds - slab * SLAB_LEN, gathered, basis, basis_t, inverse, lane_weights)
    sums = lax.all_to_all(sums, SLAB_AXES, split_axis=0, concat_axis=0, tiled=True)
    flags, scans = call(
        scan_kernel,
        (shape((BLOCKS, TILE), f32), shape((TILES + 2 * SHARE, TILE), f32)),
        [smem(), smem(), vmem()],
        (vmem(), vmem()),
        [buffer((TILES, 8, TILE), f32)],
    )(scan_bounds, tiles, own_rows)
    cleaned, sums, flags, scans = lax.optimization_barrier((cleaned, sums, flags, scans))
    returned = lax.all_to_all(cleaned, SLAB_AXES, split_axis=0, concat_axis=0, tiled=True)

    part = call(
        bin_kernel,
        shape((SUM_ROWS + TILES + 2 * SHARE, TILE), f32),
        [smem(), vmem(), vmem()],
        vmem(),
        [buffer((TILES, 2 * SHARE, TILE), f32)] * 4,
    )(tiles, sums, scans)
    sky, sky_b = call(
        sky_kernel,
        (shape((SUM_ROWS, TILE), f32), shape((SUM_ROWS, TILE), bf16)),
        [vmem()] * OBS,
        (vmem(), vmem()),
        micros=1,
    )(part, *exchange(part, "obs"))
    held = jnp.stack([sky_b] + exchange(sky_b, "q")).reshape(QUADS, TILES, SHARE, TILE)
    held = [
        lax.dynamic_index_in_dim(held, (quad - quad_of(share, group)) & 3, 0, keepdims=False)
        for share in range(QUADS)
    ]
    sky_rows = jnp.stack(held, axis=1).reshape(TILES, ROWS, TILE)
    sky_row = lax.dynamic_slice_in_dim(
        sky.reshape(TILES, SHARE, TILE), sent_row(lax.axis_index("obs"), quad, group), 1, 1
    )
    moves = [
        ((o * QUADS + q) * GROUPS + g, g * ROWS + share_of(q, g)[0] * SHARE + sent_row(o, q, g))
        for o in range(OBS)
        for q in range(QUADS)
        for g in range(GROUPS)
    ]
    sky_row, returned = lax.optimization_barrier((sky_row, returned))
    sky_own = lax.ppermute(sky_row, ALL_AXES, moves)
    out = call(
        adjoint_kernel,
        shape((1, ROWS, SAMP), f32),
        [smem(), vmem(), vmem(), vmem(), vmem()],
        hbm(),
        [
            buffer((TILES, ROWS, TILE), f32),
            *[buffer((BAND_BLOCKS * ROWS, TILE), f32)] * 6,
            buffer((ROWS, SAMP), f32),
            buffer((ROWS * BANDS, TILE), f32),
            buffer((ROWS * BANDS, TILE), f32),
            pltpu.SemaphoreType.DMA((BANDS,)),
        ],
        micros=9,
    )(tiles, flags, returned, sky_rows, taps)
    return (out, sky_own)


def solution(mesh):
    split = Mesh(mesh.devices.reshape(OBS, QUADS, GROUPS), ALL_AXES)
    placed = (
        P("obs", SLAB_AXES, None),
        P("obs", SLAB_AXES, None, None),
        P("obs", None),
        P("obs", SLAB_AXES),
        P("obs", None),
        P(),
        P(),
    )
    return jax.shard_map(
        local,
        mesh=split,
        in_specs=placed,
        out_specs=(P("obs", SLAB_AXES, None), P(None, ALL_AXES, None)),
        check_vma=False,
    )
```

```python
import functools

import jax
import jax.numpy as jnp
from jax import lax
from jax.experimental import pallas as pl
from jax.experimental.pallas import tpu as pltpu
from jax.sharding import Mesh
from jax.sharding import PartitionSpec as P

TAPS = 129
BANDS = 8
TILE = 128
WAFERS = 8
POLY = 6
NINT = 16
OBS = 4
DET = 512
SAMP = 32768
TILES = 16

QUADS = 4
GROUPS = 8
ROWS = 16
BLOCKS = SAMP // TILE
SLABS = QUADS * GROUPS
SLAB_BLOCKS = BLOCKS // SLABS
BAND_BLOCKS = BLOCKS // BANDS
HALF = TILE // 2
GROUP_AXES = ("obs", "q")
SLAB_AXES = ("q", "g")
ALL_AXES = ("obs", "q", "g")

prior_weight = 1.0
MIB = 1024 * 1024
BAND_SLABS = SLABS // BANDS
SLAB_LEN = SLAB_BLOCKS * TILE
SHARE = TILE // SLABS
SUM_ROWS = TILES * SHARE


def vmem():
    return pl.BlockSpec(memory_space=pltpu.VMEM)


def smem():
    return pl.BlockSpec(memory_space=pltpu.SMEM)


def hbm():
    return pl.BlockSpec(memory_space=pltpu.HBM)


def call(kernel, out_shape, in_specs, out_specs, scratch=(), limit=32, micros=2):
    return pl.pallas_call(
        kernel,
        out_shape=out_shape,
        in_specs=in_specs,
        out_specs=out_specs,
        scratch_shapes=list(scratch),
        compiler_params=pltpu.CompilerParams(vmem_limit_bytes=limit * MIB),
        cost_estimate=pl.CostEstimate(
            flops=0, bytes_accessed=micros * 3_000_000, transcendentals=0
        ),
    )


def share_of(quad, group):
    turn = (quad - 2 * (group & 1)) & 3
    near = turn >> 1
    return ((turn + 1) & 2) | (((group >> 2) ^ 1) ^ near), near


def quad_of(share, group):
    near = (share & 1) ^ ((group >> 2) ^ 1)
    return (2 * near + (near ^ (share >> 1)) + 2 * (group & 1)) & 3


def sent_row(obs, quad, group):
    step = (obs - (group >> 1)) & 3
    near = share_of(quad, group)[1]
    code = near * ((2 - step) & 3) + (1 - near) * (step ^ (step >> 1))
    return code ^ (2 * ((group >> 1) & 1))


def lane_ids(shape):
    return lax.broadcasted_iota(jnp.int32, shape, len(shape) - 1)


def row_ids(shape):
    return lax.broadcasted_iota(jnp.int32, shape, len(shape) - 2)


def circulant(row):
    return pltpu.roll(jnp.broadcast_to(row, (TILE, TILE)), 0, 1, stride=1, stride_axis=0)


def start(block, size):
    return pl.multiple_of(block * size, size)


def forward_kernel(
    x_ref,
    taps_ref,
    tiles_ref,
    y_ref,
    x_buf,
    taps_buf,
    shifted_a,
    shifted_b,
    summed_a,
    summed_b,
    y_buf,
    first,
    last,
    tiles,
    sems,
):
    shifted, summed = (shifted_a, shifted_b), (summed_a, summed_b)

    def x_copy(band):
        part = pl.ds(band * BAND_BLOCKS * TILE, BAND_BLOCKS * TILE)
        return pltpu.make_async_copy(x_ref.at[0, :, part], x_buf.at[:, part], sems.at[0, band])

    def y_copy(band):
        part = pl.ds(band * BAND_SLABS, BAND_SLABS)
        return pltpu.make_async_copy(y_buf.at[part], y_ref.at[part], sems.at[1, band])

    taps_copy = pltpu.make_async_copy(taps_ref, taps_buf, sems.at[0, BANDS])
    tiles_copy = pltpu.make_async_copy(tiles_ref, tiles, sems.at[1, BANDS])
    taps_copy.start()
    x_copy(0).start()
    tiles_copy.start()
    for band in range(1, BANDS):
        x_copy(band).start()
    low = lane_ids((ROWS, TILE)) < HALF
    rows, lanes = row_ids((TILE, TILE)), lane_ids((TILE, TILE))
    in_first = lanes <= rows
    on_diag = lanes == rows
    reverse = (rows == ((TILE - lanes) & (TILE - 1))).astype(jnp.float32).astype(jnp.bfloat16)
    taps_copy.wait()
    taps = taps_buf[...].astype(jnp.float32)
    front = taps[:, :, :TILE].reshape(ROWS * BANDS, TILE).astype(jnp.bfloat16)
    first[...] = jnp.dot(front, reverse, preferred_element_type=jnp.float32)
    last[...] = jnp.broadcast_to(taps[:, :, TILE:], (ROWS, BANDS, TILE)).reshape(
        ROWS * BANDS, TILE
    )
    tiles_copy.wait()
    lane = lane_ids((ROWS, TILE))
    meta = jnp.zeros((ROWS, TILE), jnp.int32)
    for block in range(SLAB_BLOCKS):
        meta = jnp.where(lane == block, tiles[0, block], meta)
    meta = meta.astype(jnp.float32).astype(jnp.bfloat16)

    def rolled(block):
        if not 0 <= block < BLOCKS:
            return jnp.zeros((ROWS, TILE), jnp.float32)
        part = x_buf[:, block * TILE : (block + 1) * TILE]
        return pltpu.roll(part.astype(jnp.float32), HALF, 1)

    def shift(band, index, before):
        here = rolled(band * BAND_BLOCKS + index)
        place = slice(index * ROWS, (index + 1) * ROWS)
        shifted[band % 2][place, :] = jnp.where(low, before, here)
        return here

    def write(band, index):
        slab, inner = band * BAND_SLABS + index // SLAB_BLOCKS, index % SLAB_BLOCKS
        part = summed[band % 2][index * ROWS : (index + 1) * ROWS, :]
        y_buf[slab, :, inner * TILE : (inner + 1) * TILE] = part.astype(jnp.bfloat16)
        if inner == 0:
            y_buf[slab, :, SLAB_LEN:] = meta

    x_copy(0).wait()
    before = rolled(-1)
    for index in range(BAND_BLOCKS):
        before = shift(0, index, before)
    for band in range(BANDS):
        if band + 1 < BANDS:
            x_copy(band + 1).wait()
        shift(band, BAND_BLOCKS, before)
        for det in range(ROWS):
            pair = det * BANDS + band
            turned = circulant(first[pair : pair + 1, :])
            end = jnp.broadcast_to(last[pair : pair + 1, :], (TILE, TILE))
            upper = jnp.where(in_first, turned, 0.0)
            lower = jnp.where(in_first, jnp.where(on_diag, end, 0.0), turned)
            kernel = jnp.concatenate([upper, lower], axis=0).astype(jnp.bfloat16)
            one = shifted[band % 2][pl.ds(det, BAND_BLOCKS, stride=ROWS), :]
            two = shifted[band % 2][pl.ds(det + ROWS, BAND_BLOCKS, stride=ROWS), :]
            window = jnp.concatenate([one, two], axis=1).astype(jnp.bfloat16)
            summed[band % 2][pl.ds(det, BAND_BLOCKS, stride=ROWS), :] = jnp.dot(
                window, kernel, preferred_element_type=jnp.float32
            )
            for index in (2 * det, 2 * det + 1):
                if band + 1 < BANDS:
                    before = shift(band + 1, index, before)
                if band > 0:
                    write(band - 1, index)
        if band > 0:
            y_copy(band - 1).start()
    for index in range(BAND_BLOCKS):
        write(BANDS - 1, index)
    y_copy(BANDS - 1).start()
    for band in range(BANDS):
        y_copy(band).wait()


def count_flags(bounds_ref, blocks, offset):
    sample = (row_ids((blocks, TILE)) + offset) * TILE + lane_ids((blocks, TILE))
    passed = jnp.zeros((blocks, TILE), jnp.int32)
    for bound in range(2 * NINT):
        passed = passed + (bounds_ref[0, bound] <= sample).astype(jnp.int32)
    return (passed & 1).astype(jnp.float32)


def fit(data, basis_t, both):
    fitted = jnp.dot(basis_t, both, preferred_element_type=jnp.float32)
    return (data.astype(jnp.float32) - fitted).astype(jnp.bfloat16)


def sums_kernel(
    bounds_ref, data_ref, basis_ref, basis_t_ref, inverse_ref, weight_ref, both_ref, sums_ref, tiles_ref, sums
):
    data = data_ref[:, :, :SLAB_LEN].reshape(DET, SLAB_LEN)
    tiles_ref[...] = data_ref[:, :, SLAB_LEN:].astype(jnp.float32)[:, 0, :].astype(jnp.int32)
    raw = jnp.dot(basis_ref[...], data, preferred_element_type=jnp.float32)
    coef = jnp.dot(
        inverse_ref[...],
        raw,
        precision=lax.Precision.HIGHEST,
        preferred_element_type=jnp.float32,
    )
    high = coef.astype(jnp.bfloat16)
    rest = (coef - high.astype(jnp.float32)).astype(jnp.bfloat16)
    both = jnp.concatenate([high, rest], axis=0)
    both_ref[...] = both
    cleaned = fit(data, basis_t_ref[...], both)
    flags = count_flags(bounds_ref, SLAB_BLOCKS, 0)
    for block in range(SLAB_BLOCKS):
        part = cleaned[:, block * TILE : (block + 1) * TILE].astype(jnp.float32)
        weighted = (part * weight_ref[...]).reshape(DET // TILE, TILE, TILE)
        total = jnp.sum(weighted, axis=0) * flags[block : block + 1, :]
        for quad in range(QUADS):
            for group in range(GROUPS):
                row = group * ROWS + share_of(quad, group)[0] * SHARE
                sums[quad * GROUPS + group, block * SHARE : (block + 1) * SHARE, :] = total[
                    row : row + SHARE, :
                ]
    sums_ref[...] = sums[...].astype(jnp.bfloat16)


def clean_kernel(data_ref, basis_t_ref, both_ref, out_ref):
    data = data_ref[:, :, :SLAB_LEN].reshape(DET, SLAB_LEN)
    out_ref[...] = fit(data, basis_t_ref[...], both_ref[...]).reshape(out_ref.shape)


def scan_kernel(bounds_ref, tiles_ref, weight_ref, flags_ref, scan_ref, acc):
    for band in range(BANDS):
        flags_ref[band * BAND_BLOCKS : (band + 1) * BAND_BLOCKS, :] = count_flags(
            bounds_ref, BAND_BLOCKS, band * BAND_BLOCKS
        )
    acc[...] = jnp.zeros_like(acc)

    def add_slab(slab, carry):
        for inner in range(SLAB_BLOCKS):
            tile = tiles_ref[slab, inner]
            row = flags_ref[pl.ds(slab * SLAB_BLOCKS + inner, 1), :]
            acc[tile] = acc[tile] + jnp.broadcast_to(row, (8, TILE))
        return carry

    lax.fori_loop(0, SLABS, add_slab, 0)
    for tile in range(TILES):
        scan_ref[tile : tile + 1, :] = acc[tile, :1, :]
    scan_ref[TILES:, :] = weight_ref[...]


def bin_kernel(tiles_ref, sums_ref, scan_ref, out_ref, *accs):
    for acc in accs:
        acc[...] = jnp.zeros_like(acc)
    upper = row_ids((2 * SHARE, TILE)) < SHARE

    def add_slabs(step, carry):
        for inner in range(SLAB_BLOCKS):
            pair = slice(inner // 2 * 2 * SHARE, (inner // 2 + 1) * 2 * SHARE)
            for which, acc in enumerate(accs):
                slab = step * len(accs) + which
                part = sums_ref[slab].astype(jnp.float32)[pair, :]
                part = jnp.where(upper, 0.0, part) if inner % 2 else jnp.where(upper, part, 0.0)
                tile = tiles_ref[slab, inner]
                acc[tile] = acc[tile] + part
        return carry

    lax.fori_loop(0, SLABS // len(accs), add_slabs, 0)
    for tile in range(TILES):
        both = sum(acc[tile] for acc in accs)
        out_ref[tile * SHARE : (tile + 1) * SHARE, :] = both[:SHARE, :] + both[SHARE:, :]
    out_ref[SUM_ROWS:, :] = scan_ref[...]


def sky_kernel(a_ref, b_ref, c_ref, d_ref, sky_ref, sky_b_ref):
    refs = (a_ref, b_ref, c_ref, d_ref)
    upper = row_ids((2 * SHARE, TILE)) < SHARE
    weights = [ref[SUM_ROWS + TILES :, :] for ref in refs]
    for pair in range(TILES // 2):
        rows = slice(pair * 2 * SHARE, (pair + 1) * 2 * SHARE)
        total = jnp.zeros((2 * SHARE, TILE), jnp.float32)
        hits = jnp.zeros((2 * SHARE, TILE), jnp.float32)
        for ref, weight in zip(refs, weights):
            total = total + ref[rows, :]
            even = ref[SUM_ROWS + 2 * pair : SUM_ROWS + 2 * pair + 1, :]
            odd = ref[SUM_ROWS + 2 * pair + 1 : SUM_ROWS + 2 * pair + 2, :]
            hits = hits + weight * jnp.where(upper, even, odd)
        sky_ref[rows, :] = total / (hits + prior_weight)
    sky_b_ref[...] = sky_ref[...].astype(jnp.bfloat16)


def adjoint_kernel(
    tiles_ref,
    flags_ref,
    data_ref,
    sky_ref,
    taps_ref,
    out_ref,
    sky,
    resid_a,
    resid_b,
    same_a,
    same_b,
    after_a,
    after_b,
    out_buf,
    first,
    last,
    sems,
):
    resid, same, after = (resid_a, resid_b), (same_a, same_b), (after_a, after_b)

    def out_copy(band):
        part = pl.ds(band * BAND_BLOCKS * TILE, BAND_BLOCKS * TILE)
        return pltpu.make_async_copy(out_buf.at[:, part], out_ref.at[0, :, part], sems.at[band])

    sky[...] = sky_ref[...].astype(jnp.float32)
    taps = taps_ref[...].astype(jnp.float32)
    first[...] = taps[:, :, :TILE].reshape(ROWS * BANDS, TILE)
    last[...] = jnp.broadcast_to(taps[:, :, TILE:], (ROWS, BANDS, TILE)).reshape(
        ROWS * BANDS, TILE
    )
    rows, lanes = row_ids((TILE, TILE)), lane_ids((TILE, TILE))
    in_first = lanes >= rows
    on_diag = lanes == rows
    low = lane_ids((ROWS, TILE)) < HALF
    zero = jnp.zeros((ROWS, TILE), jnp.float32)

    def make_residual(band, index):
        block = band * BAND_BLOCKS + index
        slab, inner = block // SLAB_BLOCKS, block % SLAB_BLOCKS
        value = data_ref[slab, :, inner * TILE : (inner + 1) * TILE].astype(jnp.float32)
        value = flags_ref[block : block + 1, :] * (value - sky[tiles_ref[slab, inner]])
        resid[band % 2][index * ROWS : (index + 1) * ROWS, :] = value

    def write_block(block, before, here):
        if block >= 0:
            out_buf[:, block * TILE : (block + 1) * TILE] = jnp.where(low, before, here)

    def join(band, index, before, spill):
        place = slice(index * ROWS, (index + 1) * ROWS)
        if index > 0:
            spill = after[band % 2][(index - 1) * ROWS : index * ROWS, :]
        here = pltpu.roll(same[band % 2][place, :] + spill, HALF, 1)
        write_block(band * BAND_BLOCKS + index - 1, before, here)
        return here

    for index in range(BAND_BLOCKS):
        make_residual(0, index)
    before, spill, next_spill = zero, zero, zero
    for band in range(BANDS + 1):
        if band >= 2:
            spill = next_spill
        if 1 <= band < BANDS:
            next_spill = after[(band - 1) % 2][(BAND_BLOCKS - 1) * ROWS :, :]
        for det in range(ROWS):
            if band < BANDS:
                pair = det * BANDS + band
                turned = circulant(first[pair : pair + 1, :])
                end = jnp.broadcast_to(last[pair : pair + 1, :], (TILE, TILE))
                upper = jnp.where(in_first, turned, 0.0)
                lower = jnp.where(in_first, jnp.where(on_diag, end, 0.0), turned)
                kernel = jnp.concatenate([upper, lower], axis=1).astype(jnp.bfloat16)
                part = resid[band % 2][pl.ds(det, BAND_BLOCKS, stride=ROWS), :]
                spread = jnp.dot(
                    part.astype(jnp.bfloat16), kernel, preferred_element_type=jnp.float32
                )
                same[band % 2][pl.ds(det, BAND_BLOCKS, stride=ROWS), :] = spread[:, :TILE]
                after[band % 2][pl.ds(det, BAND_BLOCKS, stride=ROWS), :] = spread[:, TILE:]
            for index in (2 * det, 2 * det + 1):
                if band + 1 < BANDS:
                    make_residual(band + 1, index)
                if band > 0:
                    before = join(band - 1, index, before, spill)
        if band >= 2:
            out_copy(band - 2).start()
    final = after[(BANDS - 1) % 2][(BAND_BLOCKS - 1) * ROWS :, :]
    write_block(BLOCKS - 1, before, pltpu.roll(final, HALF, 1))
    out_copy(BANDS - 1).start()
    for band in range(BANDS):
        out_copy(band).wait()


def make_basis(positions, wafer_group):
    x_pos = positions[0]
    y_pos = positions[1]
    monomials = jnp.stack(
        [jnp.ones_like(x_pos), x_pos, y_pos, x_pos * x_pos, x_pos * y_pos, y_pos * y_pos]
    )
    member = (wafer_group[None, :] == jnp.arange(WAFERS, dtype=jnp.int32)[:, None]).astype(
        jnp.float32
    )
    basis_b = (member[:, None, :] * monomials[None]).reshape(WAFERS * POLY, -1).astype(jnp.bfloat16)
    basis_f = basis_b.astype(jnp.float32)
    gram_matrix = jnp.dot(basis_f, basis_f.T, precision=lax.Precision.HIGHEST)
    factor = jnp.linalg.cholesky(gram_matrix)
    lower_inv = lax.linalg.triangular_solve(
        factor, jnp.eye(WAFERS * POLY, dtype=jnp.float32), left_side=True, lower=True
    )
    inverse = jnp.dot(lower_inv.T, lower_inv, precision=lax.Precision.HIGHEST)
    return (basis_b, inverse)


def exchange(value, axis):
    size = lax.axis_size(axis)
    return [
        lax.ppermute(value, axis, [(src, (src + step) % size) for src in range(size)])
        for step in range(1, size)
    ]


def local(timestreams, filter_taps, scan_bounds, tile_index, det_weights, positions, wafer_group):
    f32, bf16 = jnp.float32, jnp.bfloat16
    shape = jax.ShapeDtypeStruct
    buffer = pltpu.VMEM
    quad = lax.axis_index("q")
    group = lax.axis_index("g")
    slab = lax.axis_index(SLAB_AXES)
    taps = filter_taps.reshape(ROWS, BANDS, TAPS)
    filtered = call(
        forward_kernel,
        shape((SLABS, ROWS, SLAB_LEN + TILE), bf16),
        [hbm(), hbm(), hbm()],
        hbm(),
        [
            buffer((ROWS, SAMP), bf16),
            buffer((ROWS, BANDS, TAPS), bf16),
            *[buffer(((BAND_BLOCKS + 1) * ROWS, TILE), f32)] * 2,
            *[buffer((BAND_BLOCKS * ROWS, TILE), f32)] * 2,
            buffer((SLABS, ROWS, SLAB_LEN + TILE), bf16),
            buffer((ROWS * BANDS, TILE), f32),
            buffer((ROWS * BANDS, TILE), f32),
            pltpu.SMEM((1, SLAB_BLOCKS), jnp.int32),
            pltpu.SemaphoreType.DMA((2, BANDS + 1)),
        ],
        limit=60,
        micros=7,
    )(timestreams, taps, tile_index)
    gathered = lax.all_to_all(filtered, SLAB_AXES, split_axis=0, concat_axis=0, tiled=True)

    basis, inverse = make_basis(positions, wafer_group)
    basis_t = jnp.concatenate([basis, basis], axis=0).T
    weights = det_weights[0].astype(f32)
    lane_weights = jnp.broadcast_to(weights[:, None], (DET, TILE))
    row_weights = jnp.sum(weights.reshape(DET // TILE, TILE), axis=0)
    own_rows = lax.dynamic_slice_in_dim(row_weights, group * ROWS + share_of(quad, group)[0] * SHARE, SHARE)
    own_rows = jnp.broadcast_to(jnp.tile(own_rows, 2)[:, None], (2 * SHARE, TILE))
    both, sums, tiles = call(
        sums_kernel,
        (
            shape((2 * WAFERS * POLY, SLAB_LEN), bf16),
            shape((SLABS, SLAB_BLOCKS * SHARE, TILE), bf16),
            shape((SLABS, TILE), jnp.int32),
        ),
        [smem()] + [vmem()] * 5,
        (vmem(), vmem(), vmem()),
        [buffer((SLABS, SLAB_BLOCKS * SHARE, TILE), f32)],
    )(scan_bounds - slab * SLAB_LEN, gathered, basis, basis_t, inverse, lane_weights)
    cleaned = call(
        clean_kernel, shape((SLABS, ROWS, SLAB_LEN), bf16), [vmem()] * 3, vmem()
    )(gathered, basis_t, both)
    sums = lax.all_to_all(sums, SLAB_AXES, split_axis=0, concat_axis=0, tiled=True)
    flags, scans = call(
        scan_kernel,
        (shape((BLOCKS, TILE), f32), shape((TILES + 2 * SHARE, TILE), f32)),
        [smem(), smem(), vmem()],
        (vmem(), vmem()),
        [buffer((TILES, 8, TILE), f32)],
    )(scan_bounds, tiles, own_rows)
    cleaned, sums, flags, scans = lax.optimization_barrier((cleaned, sums, flags, scans))
    returned = lax.all_to_all(cleaned, SLAB_AXES, split_axis=0, concat_axis=0, tiled=True)

    part = call(
        bin_kernel,
        shape((SUM_ROWS + TILES + 2 * SHARE, TILE), f32),
        [smem(), vmem(), vmem()],
        vmem(),
        [buffer((TILES, 2 * SHARE, TILE), f32)] * 4,
    )(tiles, sums, scans)
    sky, sky_b = call(
        sky_kernel,
        (shape((SUM_ROWS, TILE), f32), shape((SUM_ROWS, TILE), bf16)),
        [vmem()] * OBS,
        (vmem(), vmem()),
        micros=1,
    )(part, *exchange(part, "obs"))
    held = jnp.stack([sky_b] + exchange(sky_b, "q")).reshape(QUADS, TILES, SHARE, TILE)
    held = [
        lax.dynamic_index_in_dim(held, (quad - quad_of(share, group)) & 3, 0, keepdims=False)
        for share in range(QUADS)
    ]
    sky_rows = jnp.stack(held, axis=1).reshape(TILES, ROWS, TILE)
    sky_row = lax.dynamic_slice_in_dim(
        sky.reshape(TILES, SHARE, TILE), sent_row(lax.axis_index("obs"), quad, group), 1, 1
    )
    moves = [
        ((o * QUADS + q) * GROUPS + g, g * ROWS + share_of(q, g)[0] * SHARE + sent_row(o, q, g))
        for o in range(OBS)
        for q in range(QUADS)
        for g in range(GROUPS)
    ]
    sky_row, returned = lax.optimization_barrier((sky_row, returned))
    sky_own = lax.ppermute(sky_row, ALL_AXES, moves)
    out = call(
        adjoint_kernel,
        shape((1, ROWS, SAMP), f32),
        [smem(), vmem(), vmem(), vmem(), vmem()],
        hbm(),
        [
            buffer((TILES, ROWS, TILE), f32),
            *[buffer((BAND_BLOCKS * ROWS, TILE), f32)] * 6,
            buffer((ROWS, SAMP), f32),
            buffer((ROWS * BANDS, TILE), f32),
            buffer((ROWS * BANDS, TILE), f32),
            pltpu.SemaphoreType.DMA((BANDS,)),
        ],
        micros=9,
    )(tiles, flags, returned, sky_rows, taps)
    return (out, sky_own)


def solution(mesh):
    split = Mesh(mesh.devices.reshape(OBS, QUADS, GROUPS), ALL_AXES)
    placed = (
        P("obs", SLAB_AXES, None),
        P("obs", SLAB_AXES, None, None),
        P("obs", None),
        P("obs", SLAB_AXES),
        P("obs", None),
        P(),
        P(),
    )
    return jax.shard_map(
        local,
        mesh=split,
        in_specs=placed,
        out_specs=(P("obs", SLAB_AXES, None), P(None, ALL_AXES, None)),
        check_vma=False,
    )
```

```python
import functools

import jax
import jax.numpy as jnp
from jax import lax
from jax.experimental import pallas as pl
from jax.experimental.pallas import tpu as pltpu
from jax.sharding import Mesh
from jax.sharding import PartitionSpec as P

TAPS = 129
BANDS = 8
TILE = 128
WAFERS = 8
POLY = 6
NINT = 16
OBS = 4
DET = 512
SAMP = 32768
TILES = 16

QUADS = 4
GROUPS = 8
ROWS = 16
BLOCKS = SAMP // TILE
SLABS = QUADS * GROUPS
SLAB_BLOCKS = BLOCKS // SLABS
BAND_BLOCKS = BLOCKS // BANDS
HALF = TILE // 2
GROUP_AXES = ("obs", "q")
SLAB_AXES = ("q", "g")
ALL_AXES = ("obs", "q", "g")

prior_weight = 1.0
MIB = 1024 * 1024
BAND_SLABS = SLABS // BANDS
SLAB_LEN = SLAB_BLOCKS * TILE
SHARE = TILE // SLABS
SUM_ROWS = TILES * SHARE


def vmem():
    return pl.BlockSpec(memory_space=pltpu.VMEM)


def smem():
    return pl.BlockSpec(memory_space=pltpu.SMEM)


def hbm():
    return pl.BlockSpec(memory_space=pltpu.HBM)


def call(kernel, out_shape, in_specs, out_specs, scratch=(), limit=32, micros=2):
    return pl.pallas_call(
        kernel,
        out_shape=out_shape,
        in_specs=in_specs,
        out_specs=out_specs,
        scratch_shapes=list(scratch),
        compiler_params=pltpu.CompilerParams(vmem_limit_bytes=limit * MIB),
        cost_estimate=pl.CostEstimate(
            flops=0, bytes_accessed=micros * 3_000_000, transcendentals=0
        ),
    )


def share_of(quad, group):
    turn = (quad - 2 * (group & 1)) & 3
    near = turn >> 1
    return ((turn + 1) & 2) | (((group >> 2) ^ 1) ^ near), near


def quad_of(share, group):
    near = (share & 1) ^ ((group >> 2) ^ 1)
    return (2 * near + (near ^ (share >> 1)) + 2 * (group & 1)) & 3


def sent_row(obs, quad, group):
    step = (obs - (group >> 1)) & 3
    near = share_of(quad, group)[1]
    code = near * ((2 - step) & 3) + (1 - near) * (step ^ (step >> 1))
    return code ^ (2 * ((group >> 1) & 1))


def lane_ids(shape):
    return lax.broadcasted_iota(jnp.int32, shape, len(shape) - 1)


def row_ids(shape):
    return lax.broadcasted_iota(jnp.int32, shape, len(shape) - 2)


def circulant(row):
    return pltpu.roll(jnp.broadcast_to(row, (TILE, TILE)), 0, 1, stride=1, stride_axis=0)


def start(block, size):
    return pl.multiple_of(block * size, size)


def forward_kernel(
    x_ref,
    taps_ref,
    tiles_ref,
    y_ref,
    x_buf,
    taps_buf,
    shifted_a,
    shifted_b,
    summed_a,
    summed_b,
    y_buf,
    first,
    last,
    tiles,
    sems,
):
    shifted, summed = (shifted_a, shifted_b), (summed_a, summed_b)

    def x_copy(band):
        part = pl.ds(band * BAND_BLOCKS * TILE, BAND_BLOCKS * TILE)
        return pltpu.make_async_copy(x_ref.at[0, :, part], x_buf.at[:, part], sems.at[0, band])

    def y_copy(band):
        part = pl.ds(band * BAND_SLABS, BAND_SLABS)
        return pltpu.make_async_copy(y_buf.at[part], y_ref.at[part], sems.at[1, band])

    taps_copy = pltpu.make_async_copy(taps_ref, taps_buf, sems.at[0, BANDS])
    tiles_copy = pltpu.make_async_copy(tiles_ref, tiles, sems.at[1, BANDS])
    taps_copy.start()
    x_copy(0).start()
    tiles_copy.start()
    for band in range(1, BANDS):
        x_copy(band).start()
    low = lane_ids((ROWS, TILE)) < HALF
    rows, lanes = row_ids((TILE, TILE)), lane_ids((TILE, TILE))
    in_first = lanes <= rows
    on_diag = lanes == rows
    reverse = (rows == ((TILE - lanes) & (TILE - 1))).astype(jnp.float32).astype(jnp.bfloat16)
    taps_copy.wait()
    taps = taps_buf[...].astype(jnp.float32)
    front = taps[:, :, :TILE].reshape(ROWS * BANDS, TILE).astype(jnp.bfloat16)
    first[...] = jnp.dot(front, reverse, preferred_element_type=jnp.float32)
    last[...] = jnp.broadcast_to(taps[:, :, TILE:], (ROWS, BANDS, TILE)).reshape(
        ROWS * BANDS, TILE
    )
    tiles_copy.wait()
    lane = lane_ids((ROWS, TILE))
    meta = jnp.zeros((ROWS, TILE), jnp.int32)
    for block in range(SLAB_BLOCKS):
        meta = jnp.where(lane == block, tiles[0, block], meta)
    meta = meta.astype(jnp.float32).astype(jnp.bfloat16)

    def rolled(block):
        if not 0 <= block < BLOCKS:
            return jnp.zeros((ROWS, TILE), jnp.float32)
        part = x_buf[:, block * TILE : (block + 1) * TILE]
        return pltpu.roll(part.astype(jnp.float32), HALF, 1)

    def shift(band, index, before):
        here = rolled(band * BAND_BLOCKS + index)
        place = slice(index * ROWS, (index + 1) * ROWS)
        shifted[band % 2][place, :] = jnp.where(low, before, here)
        return here

    def write(band, index):
        slab, inner = band * BAND_SLABS + index // SLAB_BLOCKS, index % SLAB_BLOCKS
        part = summed[band % 2][index * ROWS : (index + 1) * ROWS, :]
        y_buf[slab, :, inner * TILE : (inner + 1) * TILE] = part.astype(jnp.bfloat16)
        if inner == 0:
            y_buf[slab, :, SLAB_LEN:] = meta

    x_copy(0).wait()
    before = rolled(-1)
    for index in range(BAND_BLOCKS):
        before = shift(0, index, before)
    for band in range(BANDS):
        if band + 1 < BANDS:
            x_copy(band + 1).wait()
        shift(band, BAND_BLOCKS, before)
        for det in range(ROWS):
            pair = det * BANDS + band
            turned = circulant(first[pair : pair + 1, :])
            end = jnp.broadcast_to(last[pair : pair + 1, :], (TILE, TILE))
            upper = jnp.where(in_first, turned, 0.0)
            lower = jnp.where(in_first, jnp.where(on_diag, end, 0.0), turned)
            kernel = jnp.concatenate([upper, lower], axis=0).astype(jnp.bfloat16)
            one = shifted[band % 2][pl.ds(det, BAND_BLOCKS, stride=ROWS), :]
            two = shifted[band % 2][pl.ds(det + ROWS, BAND_BLOCKS, stride=ROWS), :]
            window = jnp.concatenate([one, two], axis=1).astype(jnp.bfloat16)
            summed[band % 2][pl.ds(det, BAND_BLOCKS, stride=ROWS), :] = jnp.dot(
                window, kernel, preferred_element_type=jnp.float32
            )
            for index in (2 * det, 2 * det + 1):
                if band + 1 < BANDS:
                    before = shift(band + 1, index, before)
                if band > 0:
                    write(band - 1, index)
        if band > 0:
            y_copy(band - 1).start()
    for index in range(BAND_BLOCKS):
        write(BANDS - 1, index)
    y_copy(BANDS - 1).start()
    for band in range(BANDS):
        y_copy(band).wait()


def count_flags(bounds_ref, blocks, offset):
    sample = (row_ids((blocks, TILE)) + offset) * TILE + lane_ids((blocks, TILE))
    passed = jnp.zeros((blocks, TILE), jnp.int32)
    for bound in range(2 * NINT):
        passed = passed + (bounds_ref[0, bound] <= sample).astype(jnp.int32)
    return (passed & 1).astype(jnp.float32)


def fit(data, basis_t, both):
    fitted = jnp.dot(basis_t, both, preferred_element_type=jnp.float32)
    return (data.astype(jnp.float32) - fitted).astype(jnp.bfloat16)


def sums_kernel(
    bounds_ref, data_ref, basis_ref, basis_t_ref, inverse_ref, weight_ref, both_ref, sums_ref, tiles_ref, sums
):
    data = data_ref[:, :, :SLAB_LEN].reshape(DET, SLAB_LEN)
    tiles_ref[...] = data_ref[:, :, SLAB_LEN:].astype(jnp.float32)[:, 0, :].astype(jnp.int32)
    raw = jnp.dot(basis_ref[...], data, preferred_element_type=jnp.float32)
    coef = jnp.dot(
        inverse_ref[...],
        raw,
        precision=lax.Precision.HIGHEST,
        preferred_element_type=jnp.float32,
    )
    high = coef.astype(jnp.bfloat16)
    rest = (coef - high.astype(jnp.float32)).astype(jnp.bfloat16)
    both = jnp.concatenate([high, rest], axis=0)
    both_ref[...] = both
    flags = count_flags(bounds_ref, SLAB_BLOCKS, 0)
    for block in range(SLAB_BLOCKS):
        if block % 2 == 0:
            pair = slice(block * TILE, (block + 2) * TILE)
            cleaned = fit(data[:, pair], basis_t_ref[...], both[:, pair])
        inner = block % 2
        part = cleaned[:, inner * TILE : (inner + 1) * TILE].astype(jnp.float32)
        weighted = (part * weight_ref[...]).reshape(DET // TILE, TILE, TILE)
        total = jnp.sum(weighted, axis=0) * flags[block : block + 1, :]
        for quad in range(QUADS):
            for group in range(GROUPS):
                row = group * ROWS + share_of(quad, group)[0] * SHARE
                sums[quad * GROUPS + group, block * SHARE : (block + 1) * SHARE, :] = total[
                    row : row + SHARE, :
                ]
    sums_ref[...] = sums[...].astype(jnp.bfloat16)


def clean_kernel(data_ref, basis_t_ref, both_ref, out_ref):
    data = data_ref[:, :, :SLAB_LEN].reshape(DET, SLAB_LEN)
    out_ref[...] = fit(data, basis_t_ref[...], both_ref[...]).reshape(out_ref.shape)


def scan_kernel(bounds_ref, tiles_ref, weight_ref, flags_ref, scan_ref, acc):
    for band in range(BANDS):
        flags_ref[band * BAND_BLOCKS : (band + 1) * BAND_BLOCKS, :] = count_flags(
            bounds_ref, BAND_BLOCKS, band * BAND_BLOCKS
        )
    acc[...] = jnp.zeros_like(acc)

    def add_slab(slab, carry):
        for inner in range(SLAB_BLOCKS):
            tile = tiles_ref[slab, inner]
            row = flags_ref[pl.ds(slab * SLAB_BLOCKS + inner, 1), :]
            acc[tile] = acc[tile] + jnp.broadcast_to(row, (8, TILE))
        return carry

    lax.fori_loop(0, SLABS, add_slab, 0)
    for tile in range(TILES):
        scan_ref[tile : tile + 1, :] = acc[tile, :1, :]
    scan_ref[TILES:, :] = weight_ref[...]


def bin_kernel(tiles_ref, sums_ref, scan_ref, out_ref, *accs):
    for acc in accs:
        acc[...] = jnp.zeros_like(acc)
    upper = row_ids((2 * SHARE, TILE)) < SHARE

    def add_slabs(step, carry):
        for inner in range(SLAB_BLOCKS):
            pair = slice(inner // 2 * 2 * SHARE, (inner // 2 + 1) * 2 * SHARE)
            for which, acc in enumerate(accs):
                slab = step * len(accs) + which
                part = sums_ref[slab].astype(jnp.float32)[pair, :]
                part = jnp.where(upper, 0.0, part) if inner % 2 else jnp.where(upper, part, 0.0)
                tile = tiles_ref[slab, inner]
                acc[tile] = acc[tile] + part
        return carry

    lax.fori_loop(0, SLABS // len(accs), add_slabs, 0)
    for tile in range(TILES):
        both = sum(acc[tile] for acc in accs)
        out_ref[tile * SHARE : (tile + 1) * SHARE, :] = both[:SHARE, :] + both[SHARE:, :]
    out_ref[SUM_ROWS:, :] = scan_ref[...]


def sky_kernel(a_ref, b_ref, c_ref, d_ref, sky_ref, sky_b_ref):
    refs = (a_ref, b_ref, c_ref, d_ref)
    upper = row_ids((2 * SHARE, TILE)) < SHARE
    weights = [ref[SUM_ROWS + TILES :, :] for ref in refs]
    for pair in range(TILES // 2):
        rows = slice(pair * 2 * SHARE, (pair + 1) * 2 * SHARE)
        total = jnp.zeros((2 * SHARE, TILE), jnp.float32)
        hits = jnp.zeros((2 * SHARE, TILE), jnp.float32)
        for ref, weight in zip(refs, weights):
            total = total + ref[rows, :]
            even = ref[SUM_ROWS + 2 * pair : SUM_ROWS + 2 * pair + 1, :]
            odd = ref[SUM_ROWS + 2 * pair + 1 : SUM_ROWS + 2 * pair + 2, :]
            hits = hits + weight * jnp.where(upper, even, odd)
        sky_ref[rows, :] = total / (hits + prior_weight)
    sky_b_ref[...] = sky_ref[...].astype(jnp.bfloat16)


def adjoint_kernel(
    tiles_ref,
    flags_ref,
    data_ref,
    sky_ref,
    taps_ref,
    out_ref,
    sky,
    resid_a,
    resid_b,
    same_a,
    same_b,
    after_a,
    after_b,
    out_buf,
    first,
    last,
    sems,
):
    resid, same, after = (resid_a, resid_b), (same_a, same_b), (after_a, after_b)

    def out_copy(band):
        part = pl.ds(band * BAND_BLOCKS * TILE, BAND_BLOCKS * TILE)
        return pltpu.make_async_copy(out_buf.at[:, part], out_ref.at[0, :, part], sems.at[band])

    sky[...] = sky_ref[...].astype(jnp.float32)
    taps = taps_ref[...].astype(jnp.float32)
    first[...] = taps[:, :, :TILE].reshape(ROWS * BANDS, TILE)
    last[...] = jnp.broadcast_to(taps[:, :, TILE:], (ROWS, BANDS, TILE)).reshape(
        ROWS * BANDS, TILE
    )
    rows, lanes = row_ids((TILE, TILE)), lane_ids((TILE, TILE))
    in_first = lanes >= rows
    on_diag = lanes == rows
    low = lane_ids((ROWS, TILE)) < HALF
    zero = jnp.zeros((ROWS, TILE), jnp.float32)

    def make_residual(band, index):
        block = band * BAND_BLOCKS + index
        slab, inner = block // SLAB_BLOCKS, block % SLAB_BLOCKS
        value = data_ref[slab, :, inner * TILE : (inner + 1) * TILE].astype(jnp.float32)
        value = flags_ref[block : block + 1, :] * (value - sky[tiles_ref[slab, inner]])
        resid[band % 2][index * ROWS : (index + 1) * ROWS, :] = value

    def write_block(block, before, here):
        if block >= 0:
            out_buf[:, block * TILE : (block + 1) * TILE] = jnp.where(low, before, here)

    def join(band, index, before, spill):
        place = slice(index * ROWS, (index + 1) * ROWS)
        if index > 0:
            spill = after[band % 2][(index - 1) * ROWS : index * ROWS, :]
        here = pltpu.roll(same[band % 2][place, :] + spill, HALF, 1)
        write_block(band * BAND_BLOCKS + index - 1, before, here)
        return here

    for index in range(BAND_BLOCKS):
        make_residual(0, index)
    before, spill, next_spill = zero, zero, zero
    for band in range(BANDS + 1):
        if band >= 2:
            spill = next_spill
        if 1 <= band < BANDS:
            next_spill = after[(band - 1) % 2][(BAND_BLOCKS - 1) * ROWS :, :]
        for det in range(ROWS):
            if band < BANDS:
                pair = det * BANDS + band
                turned = circulant(first[pair : pair + 1, :])
                end = jnp.broadcast_to(last[pair : pair + 1, :], (TILE, TILE))
                upper = jnp.where(in_first, turned, 0.0)
                lower = jnp.where(in_first, jnp.where(on_diag, end, 0.0), turned)
                kernel = jnp.concatenate([upper, lower], axis=1).astype(jnp.bfloat16)
                part = resid[band % 2][pl.ds(det, BAND_BLOCKS, stride=ROWS), :]
                spread = jnp.dot(
                    part.astype(jnp.bfloat16), kernel, preferred_element_type=jnp.float32
                )
                same[band % 2][pl.ds(det, BAND_BLOCKS, stride=ROWS), :] = spread[:, :TILE]
                after[band % 2][pl.ds(det, BAND_BLOCKS, stride=ROWS), :] = spread[:, TILE:]
            for index in (2 * det, 2 * det + 1):
                if band + 1 < BANDS:
                    make_residual(band + 1, index)
                if band > 0:
                    before = join(band - 1, index, before, spill)
            if det == 0 and band >= 2:
                out_copy(band - 2).start()
    final = after[(BANDS - 1) % 2][(BAND_BLOCKS - 1) * ROWS :, :]
    write_block(BLOCKS - 1, before, pltpu.roll(final, HALF, 1))
    out_copy(BANDS - 1).start()
    for band in range(BANDS):
        out_copy(band).wait()


def make_basis(positions, wafer_group):
    x_pos = positions[0]
    y_pos = positions[1]
    monomials = jnp.stack(
        [jnp.ones_like(x_pos), x_pos, y_pos, x_pos * x_pos, x_pos * y_pos, y_pos * y_pos]
    )
    member = (wafer_group[None, :] == jnp.arange(WAFERS, dtype=jnp.int32)[:, None]).astype(
        jnp.float32
    )
    basis_b = (member[:, None, :] * monomials[None]).reshape(WAFERS * POLY, -1).astype(jnp.bfloat16)
    basis_f = basis_b.astype(jnp.float32)
    gram_matrix = jnp.dot(basis_f, basis_f.T, precision=lax.Precision.HIGHEST)
    factor = jnp.linalg.cholesky(gram_matrix)
    lower_inv = lax.linalg.triangular_solve(
        factor, jnp.eye(WAFERS * POLY, dtype=jnp.float32), left_side=True, lower=True
    )
    inverse = jnp.dot(lower_inv.T, lower_inv, precision=lax.Precision.HIGHEST)
    return (basis_b, inverse)


def exchange(value, axis):
    size = lax.axis_size(axis)
    return [
        lax.ppermute(value, axis, [(src, (src + step) % size) for src in range(size)])
        for step in range(1, size)
    ]


def local(timestreams, filter_taps, scan_bounds, tile_index, det_weights, positions, wafer_group):
    f32, bf16 = jnp.float32, jnp.bfloat16
    shape = jax.ShapeDtypeStruct
    buffer = pltpu.VMEM
    quad = lax.axis_index("q")
    group = lax.axis_index("g")
    slab = lax.axis_index(SLAB_AXES)
    taps = filter_taps.reshape(ROWS, BANDS, TAPS)
    filtered = call(
        forward_kernel,
        shape((SLABS, ROWS, SLAB_LEN + TILE), bf16),
        [hbm(), hbm(), hbm()],
        hbm(),
        [
            buffer((ROWS, SAMP), bf16),
            buffer((ROWS, BANDS, TAPS), bf16),
            *[buffer(((BAND_BLOCKS + 1) * ROWS, TILE), f32)] * 2,
            *[buffer((BAND_BLOCKS * ROWS, TILE), f32)] * 2,
            buffer((SLABS, ROWS, SLAB_LEN + TILE), bf16),
            buffer((ROWS * BANDS, TILE), f32),
            buffer((ROWS * BANDS, TILE), f32),
            pltpu.SMEM((1, SLAB_BLOCKS), jnp.int32),
            pltpu.SemaphoreType.DMA((2, BANDS + 1)),
        ],
        limit=60,
        micros=7,
    )(timestreams, taps, tile_index)
    gathered = lax.all_to_all(filtered, SLAB_AXES, split_axis=0, concat_axis=0, tiled=True)

    basis, inverse = make_basis(positions, wafer_group)
    basis_t = jnp.concatenate([basis, basis], axis=0).T
    weights = det_weights[0].astype(f32)
    lane_weights = jnp.broadcast_to(weights[:, None], (DET, TILE))
    row_weights = jnp.sum(weights.reshape(DET // TILE, TILE), axis=0)
    own_rows = lax.dynamic_slice_in_dim(row_weights, group * ROWS + share_of(quad, group)[0] * SHARE, SHARE)
    own_rows = jnp.broadcast_to(jnp.tile(own_rows, 2)[:, None], (2 * SHARE, TILE))
    both, sums, tiles = call(
        sums_kernel,
        (
            shape((2 * WAFERS * POLY, SLAB_LEN), bf16),
            shape((SLABS, SLAB_BLOCKS * SHARE, TILE), bf16),
            shape((SLABS, TILE), jnp.int32),
        ),
        [smem()] + [vmem()] * 5,
        (vmem(), vmem(), vmem()),
        [buffer((SLABS, SLAB_BLOCKS * SHARE, TILE), f32)],
    )(scan_bounds - slab * SLAB_LEN, gathered, basis, basis_t, inverse, lane_weights)
    cleaned = call(
        clean_kernel, shape((SLABS, ROWS, SLAB_LEN), bf16), [vmem()] * 3, vmem()
    )(gathered, basis_t, both)
    sums = lax.all_to_all(sums, SLAB_AXES, split_axis=0, concat_axis=0, tiled=True)
    flags, scans = call(
        scan_kernel,
        (shape((BLOCKS, TILE), f32), shape((TILES + 2 * SHARE, TILE), f32)),
        [smem(), smem(), vmem()],
        (vmem(), vmem()),
        [buffer((TILES, 8, TILE), f32)],
    )(scan_bounds, tiles, own_rows)
    cleaned, sums, flags, scans = lax.optimization_barrier((cleaned, sums, flags, scans))
    returned = lax.all_to_all(cleaned, SLAB_AXES, split_axis=0, concat_axis=0, tiled=True)

    part = call(
        bin_kernel,
        shape((SUM_ROWS + TILES + 2 * SHARE, TILE), f32),
        [smem(), vmem(), vmem()],
        vmem(),
        [buffer((TILES, 2 * SHARE, TILE), f32)] * 4,
    )(tiles, sums, scans)
    sky, sky_b = call(
        sky_kernel,
        (shape((SUM_ROWS, TILE), f32), shape((SUM_ROWS, TILE), bf16)),
        [vmem()] * OBS,
        (vmem(), vmem()),
        micros=1,
    )(part, *exchange(part, "obs"))
    held = jnp.stack([sky_b] + exchange(sky_b, "q")).reshape(QUADS, TILES, SHARE, TILE)
    held = [
        lax.dynamic_index_in_dim(held, (quad - quad_of(share, group)) & 3, 0, keepdims=False)
        for share in range(QUADS)
    ]
    sky_rows = jnp.stack(held, axis=1).reshape(TILES, ROWS, TILE)
    sky_row = lax.dynamic_slice_in_dim(
        sky.reshape(TILES, SHARE, TILE), sent_row(lax.axis_index("obs"), quad, group), 1, 1
    )
    moves = [
        ((o * QUADS + q) * GROUPS + g, g * ROWS + share_of(q, g)[0] * SHARE + sent_row(o, q, g))
        for o in range(OBS)
        for q in range(QUADS)
        for g in range(GROUPS)
    ]
    sky_row, returned = lax.optimization_barrier((sky_row, returned))
    sky_own = lax.ppermute(sky_row, ALL_AXES, moves)
    out = call(
        adjoint_kernel,
        shape((1, ROWS, SAMP), f32),
        [smem(), vmem(), vmem(), vmem(), vmem()],
        hbm(),
        [
            buffer((TILES, ROWS, TILE), f32),
            *[buffer((BAND_BLOCKS * ROWS, TILE), f32)] * 6,
            buffer((ROWS, SAMP), f32),
            buffer((ROWS * BANDS, TILE), f32),
            buffer((ROWS * BANDS, TILE), f32),
            pltpu.SemaphoreType.DMA((BANDS,)),
        ],
        micros=9,
    )(tiles, flags, returned, sky_rows, taps)
    return (out, sky_own)


def solution(mesh):
    split = Mesh(mesh.devices.reshape(OBS, QUADS, GROUPS), ALL_AXES)
    placed = (
        P("obs", SLAB_AXES, None),
        P("obs", SLAB_AXES, None, None),
        P("obs", None),
        P("obs", SLAB_AXES),
        P("obs", None),
        P(),
        P(),
    )
    return jax.shard_map(
        local,
        mesh=split,
        in_specs=placed,
        out_specs=(P("obs", SLAB_AXES, None), P(None, ALL_AXES, None)),
        check_vma=False,
    )
```
